128 devices in a mesh: slab: 128 (over x, z, y, core).
Axes of the slice: x: 4, y: 4, z: 4, core: 2. Of those that a mesh axis runs over, the one named last changes fastest.
Arguments:
- positions: float32 [16384, 3, 128], P('slab'), may hold values from -1.2 to 1.2
- velocity: float32 [16384, 3, 128], P('slab'), may hold values from -6 to 6
- masses: float32 [16384, 128], P('slab'), may hold values from 0.5 to 2
- counts: int32 [16384], P('slab'), may hold values from 16 to 128, as said below
- pair_home: int32 [81920], P('slab'), may hold values from 0 to 127, as said below
- pair_far: int32 [81920], P('slab'), may hold values from 0 to 127, as said below
- pair_owner: int32 [81920], P('slab'), may hold values from 0 to 1, as said below
- cot_x: float32 [16384, 3, 128], P('slab'), may hold values from -6 to 6
- cot_v: float32 [16384, 3, 128], P('slab'), may hold values from -6 to 6
Outputs:
- new_x: float32 [16384, 3, 128], P('slab')
- new_v: float32 [16384, 3, 128], P('slab')
- grad_x: float32 [16384, 3, 128], P('slab')
- grad_v: float32 [16384, 3, 128], P('slab')
- grad_m: float32 [16384, 128], P('slab')
The draws below stay inside these ranges and needn't reach their ends.
Inputs may be any that keep to these rules, and one draw needn't show every extreme that they name: counts[b] slots of block b hold particles, the rest are padding. `pair_home`: entries k * 640 to (k + 1) * 640 - 1 belong to slab k. Where pair_owner is 0, pair_far differs from pair_home. `pair_owner`: always 0 on the last slab.
All inputs are finite; a program needn't handle non-finite values.
Results may differ from the reference program's by a relative error of at most 0.00002.
Values sent between devices are 32-bit elements; how exact they have to be, the bound alone decides.
A program may use at most 64 MiB of HBM per device.

```python
import math
import jax
import jax.numpy as jnp
from jax import lax

PB = 128
NB = 128
PAIRS = 640
BLOCKS = 16384
N_SLAB = 128


def pair_tables(key):
    slab_count = BLOCKS // NB
    entry_idx = jnp.arange(slab_count * PAIRS, dtype=jnp.int32)
    slab_idx = entry_idx // PAIRS
    shape_all = (slab_count * PAIRS,)
    home_block = jax.random.randint(jax.random.fold_in(key, 11), shape_all, 0, NB, dtype=jnp.int32)
    next_flag = jax.random.randint(jax.random.fold_in(key, 12), shape_all, 0, 2, dtype=jnp.int32)
    owner_flag = jnp.where(slab_idx == slab_count - 1, 0, next_flag)
    offset_draw = jax.random.randint(jax.random.fold_in(key, 13), shape_all, 1, NB, dtype=jnp.int32)
    any_block = jax.random.randint(jax.random.fold_in(key, 14), shape_all, 0, NB, dtype=jnp.int32)
    far_block = jnp.where(owner_flag == 0, (home_block + offset_draw) % NB, any_block)
    return (home_block, far_block, owner_flag)


def draw_pair_home(key, part):
    tables_out = pair_tables(key)
    return tables_out[0]


def draw_pair_far(key, part):
    tables_out = pair_tables(key)
    return tables_out[1]


def draw_pair_owner(key, part):
    tables_out = pair_tables(key)
    return tables_out[2]


def draw_counts(key, part):
    key = jax.random.fold_in(key, 5)
    slab_count = BLOCKS // NB
    block_idx = jnp.arange(BLOCKS, dtype=jnp.int32)
    slab_idx = block_idx // NB
    ceiling = 32 + 96 * (slab_count - slab_idx) // slab_count
    drawn = jax.random.randint(key, (BLOCKS,), ceiling // 2, ceiling + 1, dtype=jnp.int32)
    return jnp.where(block_idx == 0, PB, drawn)


def shard_levels(key, extent, pieces, smallest, high):
    def one(axis_at, shards_of):
        steps = jax.random.uniform(jax.random.fold_in(jax.random.fold_in(key, 6), axis_at), (shards_of,), jnp.float32, smallest / len(pieces), high / len(pieces))
        return jnp.repeat(jnp.exp(steps), extent[axis_at] // shards_of).reshape((-1,) + (1,) * (len(extent) - axis_at - 1))

    factor_of = one(*pieces[0])
    for cut in pieces[1:]:
        factor_of = factor_of * one(*cut)
    return factor_of


def scatter_about(rng, dims, scale, most, cuts=(), kind=jnp.bfloat16):
    loudness = shard_levels(rng, dims, cuts, -0.22, 0.18) if cuts else 1.0
    result = jax.random.normal(rng, dims, jnp.float32) * scale * loudness
    return jnp.minimum(jnp.maximum(result, -most), most).astype(kind)


def setup_inputs(seed: int = 0) -> dict:
    key_list = jax.random.split(jax.random.key(seed), 10)
    return {
        "positions": scatter_about(key_list[0], (BLOCKS, 3, PB), 0.3, 1.2, ((0, 128),), jnp.float32),
        "velocity": scatter_about(key_list[1], (BLOCKS, 3, PB), 1.0, 6.0, ((0, 128),), jnp.float32),
        "masses": jnp.clip(jnp.exp(math.log(2.0) - 1.3862944 * jax.random.uniform(key_list[2], (BLOCKS, PB), jnp.float32) ** shard_levels(key_list[2], (BLOCKS, PB), ((0, 128),), -0.2, 0.2)), 0.5, 2.0),
        "counts": draw_counts(jax.random.fold_in(key_list[9], 71), 0),
        "pair_home": draw_pair_home(jax.random.fold_in(key_list[9], 71), 0),
        "pair_far": draw_pair_far(jax.random.fold_in(key_list[9], 71), 0),
        "pair_owner": draw_pair_owner(jax.random.fold_in(key_list[9], 71), 0),
        "cot_x": scatter_about(key_list[7], (BLOCKS, 3, PB), 1.0, 6.0, ((0, 128),), jnp.float32),
        "cot_v": scatter_about(key_list[8], (BLOCKS, 3, PB), 1.0, 6.0, ((0, 128),), jnp.float32),
    }


DT = 0.1
VISCOSITY = 0.5
STIFFNESS = 0.5
RHO_FLOOR = 0.5
GRAVITY = 1.0
tile_batch = 32

def separation(a, b):
    offsets = a[:, 0:3, :, None] - b[:, 0:3, None, :]
    return (offsets, lax.optimization_barrier(jnp.sum(offsets * offsets, axis=1)))

def density_tile(a, b):
    offsets, square = separation(a, b)
    inside = jnp.maximum(1.0 - square, 0.0)
    kernel = inside * inside * inside
    to_a = lax.optimization_barrier(jnp.sum(kernel * b[:, 6, None, :], axis=2)) / a.shape[2]
    to_b = lax.optimization_barrier(jnp.sum(kernel * a[:, 6, :, None], axis=1)) / a.shape[2]
    return (to_a[:, None, :], to_b[:, None, :])

def force_tile(a, b):
    offsets, square = separation(a, b)
    inside = jnp.maximum(1.0 - square, 0.0)
    falloff = inside * inside
    kernel = falloff * inside
    pressure = 6.0 * (a[:, 7, :, None] + b[:, 7, None, :]) * falloff
    damping = VISCOSITY * kernel
    push_a = pressure * b[:, 6, None, :]
    push_b = pressure * a[:, 6, :, None]
    damp_a = damping * (b[:, 6] * b[:, 8])[:, None, :]
    damp_b = damping * (a[:, 6] * a[:, 8])[:, :, None]
    to_a = lax.optimization_barrier(jnp.sum(push_a[:, None] * offsets, axis=3)) + lax.optimization_barrier(jnp.sum(damp_a[:, None] * b[:, 3:6, None, :], axis=3)) - a[:, 3:6] * lax.optimization_barrier(jnp.sum(damp_a, axis=2))[:, None, :]
    to_b = -lax.optimization_barrier(jnp.sum(push_b[:, None] * offsets, axis=2)) + lax.optimization_barrier(jnp.sum(damp_b[:, None] * a[:, 3:6, :, None], axis=2)) - b[:, 3:6] * lax.optimization_barrier(jnp.sum(damp_b, axis=1))[:, None, :]
    return (to_a / a.shape[2], to_b / a.shape[2])

def eos_state(density):
    bounded = jnp.sqrt(density * density + RHO_FLOOR * RHO_FLOOR)
    return (STIFFNESS * (bounded * bounded * bounded - 1.0) / (bounded * bounded), 1.0 / bounded)

def grouped(first_idx, second_idx, first_w, second_w):
    group_size = math.gcd(first_idx.shape[0], tile_batch)
    return (first_idx.reshape(-1, group_size), second_idx.reshape(-1, group_size), first_w.reshape(-1, group_size), second_w.reshape(-1, group_size))

def accumulate(tile_fn, table_in, first_idx, second_idx, first_w, second_w, height, channels):

    def one_group(running, group):
        lead_idx, other_idx, lead_w, other_w = group
        to_a, to_b = tile_fn(table_in[lead_idx], table_in[other_idx])
        running = running.at[lead_idx].add(to_a * lead_w[:, None, None])
        running = running.at[other_idx].add(to_b * other_w[:, None, None])
        return (running, None)
    initial = jnp.zeros((height, channels, table_in.shape[2]), jnp.float32)
    return lax.scan(one_group, initial, grouped(first_idx, second_idx, first_w, second_w))[0]

def pull_back(tile_fn, table_in, first_idx, second_idx, first_w, second_w, cotangent):

    def one_group(gradient, group):
        lead_idx, other_idx, lead_w, other_w = group
        _, backward = jax.vjp(tile_fn, table_in[lead_idx], table_in[other_idx])
        grad_a, grad_b = backward((cotangent[lead_idx] * lead_w[:, None, None], cotangent[other_idx] * other_w[:, None, None]))
        gradient = gradient.at[lead_idx].add(grad_a).at[other_idx].add(grad_b)
        return (gradient, None)
    initial = jnp.zeros(table_in.shape, jnp.float32)
    return lax.scan(one_group, initial, grouped(first_idx, second_idx, first_w, second_w))[0]

def reference(positions, velocity, masses, counts, pair_home, pair_far, pair_owner, cot_x, cot_v):
    blocks = positions.shape[0]
    occupied = (lax.broadcasted_iota(jnp.int32, masses.shape, 1) < counts[:, None]).astype(jnp.float32)
    live_mass = masses * occupied
    particle_table = jnp.concatenate([positions, velocity, live_mass[:, None, :]], axis=1)
    own_block = jnp.arange(blocks, dtype=jnp.int32)
    slab_of = jnp.arange(N_SLAB * PAIRS, dtype=jnp.int32) // PAIRS
    first_idx = jnp.concatenate([own_block, slab_of * NB + pair_home])
    second_idx = jnp.concatenate([own_block, (slab_of + pair_owner) * NB + pair_far])
    first_w = jnp.ones(first_idx.shape, jnp.float32)
    second_w = jnp.concatenate([jnp.zeros((blocks,), jnp.float32), jnp.ones((N_SLAB * PAIRS,), jnp.float32)])
    density = accumulate(density_tile, particle_table, first_idx, second_idx, first_w, second_w, blocks, 1)[:, 0]
    (pressure_term, inverse), eos_back = jax.vjp(eos_state, density)
    table_two = jnp.concatenate([particle_table, pressure_term[:, None, :], inverse[:, None, :]], axis=1)
    acceleration = accumulate(force_tile, table_two, first_idx, second_idx, first_w, second_w, blocks, 3)
    acceleration = acceleration + jnp.array([0.0, 0.0, -GRAVITY], jnp.float32)[None, :, None]
    new_v = velocity + DT * acceleration
    new_x = positions + DT * new_v
    grad_new_v = cot_v + DT * cot_x
    grad_two = pull_back(force_tile, table_two, first_idx, second_idx, first_w, second_w, DT * grad_new_v)
    grad_density = eos_back((grad_two[:, 7], grad_two[:, 8]))[0]
    grad_one = pull_back(density_tile, particle_table, first_idx, second_idx, first_w, second_w, grad_density[:, None, :])
    grad_x = cot_x + grad_two[:, 0:3] + grad_one[:, 0:3]
    grad_v = grad_new_v + grad_two[:, 3:6]
    grad_m = (grad_two[:, 6] + grad_one[:, 6]) * occupied
    return (new_x, new_v, grad_x, grad_v, grad_m)
```

```python
import functools

import jax
import jax.numpy as jnp
from jax import lax
from jax.experimental import pallas as pl
from jax.experimental.pallas import tpu as pltpu
from jax.sharding import PartitionSpec as P

DT = 0.1
GRAVITY = 1.0
KAPPA = 1.0 / 128.0
LEAD = 64
SHORT = 32
LONG = 16
F32 = jnp.float32
BF16 = jnp.bfloat16


def dot(a, b, ca=1, cb=0):
    return lax.dot_general(a, b, (((ca,), (cb,)), ((), ())), preferred_element_type=F32)


def rounded(value):
    return value.astype(BF16).astype(F32)


def halves(value):
    high = rounded(value)
    return high, value - high


def thirds(value):
    high = rounded(value)
    rest = value - high
    middle = rounded(rest)
    return high, middle, rest - middle


def source_features(e):
    h, m, l = thirds(e)
    return jnp.concatenate([h, h, m, h, l, m], axis=0).astype(BF16)


def target_features(r):
    h, m, l = thirds(r)
    return jnp.concatenate([h, m, h, l, h, m], axis=0).astype(BF16)


def row_index():
    return lax.broadcasted_iota(jnp.int32, (8, 128), 0)


def basis(a):
    return jnp.where(row_index() < 5, a, 0.0)


def target_basis(a):
    row = row_index()
    return jnp.where(
        row == 0, 1.0 - a[1:2], jnp.where(row == 1, -1.0, jnp.where(row < 5, 2.0 * a, 0.0))
    )


def list_kernel(home, far, owner, p_home, p_far, p_owner, entries, count):
    pairs = home.shape[0]
    blocks = 128
    dead = blocks * 512 + blocks

    def own(k, at):
        h, f, o = home[k], far[k], owner[k]
        entries[at] = h * 512 + f + blocks + o * blocks
        entries[at + 1] = f * 512 + h + blocks
        return at + 2 - o

    def previous(k, at):
        entries[at] = p_far[k] * 512 + p_home[k]
        return at + p_owner[k]

    def self_pair(b, at):
        entries[LEAD + b] = b * 512 + b + blocks
        return at

    lax.fori_loop(0, blocks, self_pair, 0, unroll=8)
    for extra in range(LEAD):
        entries[extra] = dead
    at = lax.fori_loop(0, pairs, own, LEAD + blocks, unroll=8)
    at = lax.fori_loop(0, pairs, previous, at, unroll=8)
    for extra in range(2 * LEAD):
        entries[at + extra] = dead
    count[0] = at - LEAD


def make_list(home, far, owner, p_home, p_far, p_owner):
    pairs = home.shape[0]
    smem = pl.BlockSpec(memory_space=pltpu.SMEM)
    return pl.pallas_call(
        list_kernel,
        out_shape=(
            jax.ShapeDtypeStruct((128 + 3 * pairs + 4 * LEAD,), jnp.int32),
            jax.ShapeDtypeStruct((8,), jnp.int32),
        ),
        in_specs=[smem] * 6,
        out_specs=(smem, smem),
        name="tile_list",
    )(home, far, owner, p_home, p_far, p_owner)


def group_at(entries, t, size):
    found = [entries[LEAD + t * size + k] for k in range(size)]
    return [(lax.shift_right_logical(e, 9), lax.bitwise_and(e, 511)) for e in found]


def group_loop(count, size, stages, step):
    groups = lax.shift_right_logical(count[0] + (size - 1), size.bit_length() - 1)

    def body(t, carry):
        step(t)
        return carry

    lax.fori_loop(0, groups + stages - 1, body, 0)


def two_tiles(sources, targets, one, two):
    (x0, y0), (x1, y1) = one, two
    lhs = jnp.concatenate([sources[y0], sources[y1]], axis=0)
    zero = jnp.zeros((48, 128), BF16)
    rhs = jnp.concatenate(
        [
            jnp.concatenate([targets[x0], zero], axis=1),
            jnp.concatenate([zero, targets[x1]], axis=1),
        ],
        axis=0,
    )
    return jnp.maximum(dot(lhs, rhs, 0, 0), 0.0)


def make_tiles(sources, targets, tiles, k, distances):
    distances[k // 2] = two_tiles(sources, targets, tiles[k], tiles[k + 1])


def for_blocks(blocks, fn, unroll=4):
    def body(b, carry):
        fn(b)
        return carry

    lax.fori_loop(0, blocks, body, 0, unroll=unroll)


def density_kernel(entries, count, a_prev, a_own, a_next, out, sources, targets, acc, distances):
    blocks = a_own.shape[0]
    for part, a_ref in enumerate((a_prev, a_own, a_next)):

        def prepare(b, part=part, a_ref=a_ref):
            a = a_ref[b]
            sources[part * blocks + b] = source_features(basis(a) * a[6:7])
            if part == 1:
                targets[b] = target_features(target_basis(a))
                acc[b] = jnp.zeros((8, 128), F32)

        for_blocks(blocks, prepare)
    targets[blocks] = jnp.zeros((48, 128), BF16)
    acc[blocks] = jnp.zeros((8, 128), F32)

    def step(t):
        newer, older = group_at(entries, t, SHORT), group_at(entries, t - 1, SHORT)
        for k in range(0, SHORT, 2):
            c = distances[k // 2]
            mass_kernel = c * c * c
            total = jnp.sum(mass_kernel.reshape(16, 8, 256), axis=0)
            for j in range(2):
                x = older[k + j][0]
                acc[x] = acc[x] + total[:, 128 * j : 128 * j + 128]
            make_tiles(sources, targets, newer, k, distances)

    group_loop(count, SHORT, 2, step)

    def finish(b):
        density = KAPPA * jnp.sum(acc[b], axis=0, keepdims=True)
        square = density * density + 0.25
        inverse = lax.rsqrt(square)
        inverse = inverse * (1.5 - 0.5 * square * inverse * inverse)
        bounded = square * inverse
        pressure = 0.5 * (bounded - inverse * inverse)
        row = lax.broadcasted_iota(jnp.int32, (4, 128), 0)
        out[b] = jnp.where(
            row == 0, pressure, jnp.where(row == 1, inverse, jnp.where(row == 2, density, bounded))
        )

    for_blocks(blocks, finish)


def run_density(entries, count, a_prev, a_own, a_next):
    blocks = a_own.shape[0]
    smem = pl.BlockSpec(memory_space=pltpu.SMEM)
    vmem = pl.BlockSpec(memory_space=pltpu.VMEM)
    return pl.pallas_call(
        density_kernel,
        out_shape=jax.ShapeDtypeStruct((blocks, 4, 128), F32),
        in_specs=[smem, smem, vmem, vmem, vmem],
        out_specs=vmem,
        scratch_shapes=[
            pltpu.VMEM((3 * blocks, 48, 128), BF16),
            pltpu.VMEM((blocks + 1, 48, 128), BF16),
            pltpu.VMEM((blocks + 1, 8, 128), F32),
            pltpu.VMEM((SHORT // 2, 128, 256), F32),
        ],
        compiler_params=pltpu.CompilerParams(vmem_limit_bytes=24 << 20),
        cost_estimate=pl.CostEstimate(flops=10**9, bytes_accessed=2 * 10**6, transcendentals=0),
        name="density",
    )(entries, count, a_prev, a_own, a_next)


F_ROWS = 72
C_ROWS = 64


def stacked(groups):
    value = jnp.concatenate(groups, axis=0)
    high, low = halves(value)
    return jnp.concatenate([high, low], axis=0).astype(BF16)


def split_rows(tile):
    high, low = halves(tile)
    return jnp.concatenate([high.astype(BF16), low.astype(BF16)], axis=0)


def matrix_sum(channels, right):
    both = dot(jnp.concatenate([channels, channels], axis=1), right)
    rows = channels.shape[0] // 2
    return both[:rows] + both[rows:]


def force_kernel(
    entries, count, a_prev, a_own, a_next, b_prev, b_own, b_next, q_prev, q_own, q_next,
    cot_x, out, h_out, sources, targets, f_channels, c_channels, acc,
    distances, f_right, c_right,
):
    blocks = a_own.shape[0]
    row = row_index()
    parts = ((a_prev, b_prev, q_prev), (a_own, b_own, q_own), (a_next, b_next, q_next))
    for part, (a_ref, b_ref, q_ref) in enumerate(parts):

        def prepare(b, part=part, a_ref=a_ref, b_ref=b_ref, q_ref=q_ref):
            at = part * blocks + b
            a = a_ref[b]
            vg_rows = b_ref[b]
            p, q = q_ref[b, 0:1], q_ref[b, 1:2]
            e = basis(a)
            x = [a[2 + k : 3 + k] for k in range(3)]
            v = [vg_rows[k : k + 1] for k in range(3)]
            g = [vg_rows[3 + k : 4 + k] for k in range(3)]
            mass = a[5:6]
            u = mass * q
            vg = v[0] * g[0] + v[1] * g[1] + v[2] * g[2]
            xg = x[0] * g[0] + x[1] * g[1] + x[2] * g[2]
            sources[at] = source_features(e)
            e_one = jnp.where(row == 5, p, e)
            e_two = jnp.where(
                row >= 5, p * pltpu.roll(e, 3, 0), jnp.where(row == 1, p, e)
            )
            f_channels[at] = stacked(
                [g[k] * e_one for k in range(3)]
                + [jnp.where(row == 5, p * xg, vg * e_one), u * e_one]
                + [(u * v[k]) * e_one for k in range(3)]
                + [mass * e_two]
            )
            me = mass * e_two
            c_channels[at] = stacked(
                [me] + [x[k] * me for k in range(3)] + [g[k] * e_two for k in range(3)]
                + [xg * e_two]
            )
            if part == 1:
                targets[b] = target_features(target_basis(a))
                acc[b] = jnp.zeros((F_ROWS + C_ROWS, 128), F32)

        for_blocks(blocks, prepare, unroll=2)
    targets[blocks] = jnp.zeros((48, 128), BF16)
    acc[blocks] = jnp.zeros((F_ROWS + C_ROWS, 128), F32)

    def step(t):
        newest, oldest = group_at(entries, t, LONG), group_at(entries, t - 2, LONG)
        for k in range(0, LONG, 2):
            for j in range(2):
                x, y = oldest[k + j]
                f_sum = matrix_sum(f_channels[y], f_right[k + j])
                c_sum = matrix_sum(c_channels[y], c_right[k + j])
                acc[x, 0:F_ROWS] = acc[x, 0:F_ROWS] + f_sum
                acc[x, F_ROWS : F_ROWS + C_ROWS] = acc[x, F_ROWS : F_ROWS + C_ROWS] + c_sum
            for j in range(2):
                c = distances[k // 2, :, 128 * j : 128 * j + 128]
                f_right[k + j] = split_rows(c * c)
                c_right[k + j] = split_rows(c)
            make_tiles(sources, targets, newest, k, distances)

    group_loop(count, LONG, 3, step)

    def finish(b):
        a = a_own[b]
        vg_rows = b_own[b]
        p, q = q_own[b, 0:1], q_own[b, 1:2]
        density, bounded = q_own[b, 2:3], q_own[b, 3:4]
        x = [a[2 + k : 3 + k] for k in range(3)]
        v = [vg_rows[k : k + 1] for k in range(3)]
        g = [vg_rows[3 + k : 4 + k] for k in range(3)]
        mass = a[5:6]
        u = mass * q
        vg = v[0] * g[0] + v[1] * g[1] + v[2] * g[2]
        xg = x[0] * g[0] + x[1] * g[1] + x[2] * g[2]
        r = target_basis(a)

        def group(k):
            return acc[b, 8 * k : 8 * k + 8]

        s_g = [group(k) for k in range(3)]
        s_vg, s_u = group(3), group(4)
        s_uv = [group(5 + k) for k in range(3)]
        s_m = group(8)
        c_m = group(9)
        c_mx = [group(10 + k) for k in range(3)]
        c_g = [group(13 + k) for k in range(3)]
        c_xg = group(16)

        def weighted(s):
            return jnp.sum(s * r, axis=0, keepdims=True)

        m0, m1 = s_m[0:1], s_m[1:2]
        mx = [s_m[2 + k : 3 + k] for k in range(3)]
        mpx = [s_m[5 + k : 6 + k] for k in range(3)]
        g0 = [s_g[k][0:1] for k in range(3)]
        g1 = [s_g[k][5:6] for k in range(3)]
        xg0 = s_g[0][2:3] + s_g[1][3:4] + s_g[2][4:5]
        xg1 = s_vg[5:6]
        xm = [x[k] * m0 - mx[k] for k in range(3)]
        energy = weighted(s_vg - (v[0] * s_g[0] + v[1] * s_g[1] + v[2] * s_g[2]))
        xdg0 = x[0] * g0[0] + x[1] * g0[1] + x[2] * g0[2]
        xdg1 = x[0] * g1[0] + x[1] * g1[1] + x[2] * g1[2]
        grad_m = KAPPA * (-6.0 * (p * (xdg0 - xg0) + xdg1 - xg1) - 0.5 * q * energy)
        grad_q = (-0.5 * KAPPA) * mass * energy
        grad_p = (6.0 * KAPPA) * (
            g[0] * xm[0] + g[1] * xm[1] + g[2] * xm[2] - mass * (xdg0 - xg0)
        )
        f_v = (
            u * (v[0] * s_g[0] + v[1] * s_g[1] + v[2] * s_g[2] - s_vg)
            + g[0] * s_uv[0] + g[1] * s_uv[1] + g[2] * s_uv[2] - vg * s_u
        )
        c_d = (
            xg * c_m - (g[0] * c_mx[0] + g[1] * c_mx[1] + g[2] * c_mx[2])
            + mass * (c_xg - (x[0] * c_g[0] + x[1] * c_g[1] + x[2] * c_g[2]))
        )
        c_d0 = p * c_d[0:1] + c_d[1:2]
        rows = []
        new_v, grad_v, grad_x = [], [], []
        for k in range(3):
            accel = KAPPA * (
                6.0 * (p * xm[k] + x[k] * m1 - mpx[k])
                + 0.5 * weighted(s_uv[k] - v[k] * s_u)
            )
            if k == 2:
                accel = accel - GRAVITY
            new_v.append(v[k] + DT * accel)
            grad_v.append(
                g[k] * (1.0 / DT) - (0.5 * KAPPA) * weighted(g[k] * s_u - u * s_g[k])
            )
            through = 24.0 * (
                x[k] * c_d0 - (p * c_d[2 + k : 3 + k] + c_d[5 + k : 6 + k])
            ) + 3.0 * (x[k] * f_v[0:1] - f_v[2 + k : 3 + k])
            direct = 6.0 * (g[k] * (p * m0 + m1) - mass * (p * g0[k] + g1[k]))
            grad_x.append(cot_x[b, k : k + 1] + KAPPA * (direct - through))
        new_x = [x[k] + DT * new_v[k] for k in range(3)]
        inv = q
        h = (density * inv) * (
            0.5 * (1.0 + 2.0 * inv * inv * inv) * grad_p - inv * inv * grad_q
        )
        rows = new_x + new_v + grad_v + grad_x + xm + [grad_m]
        for k, value in enumerate(rows):
            out[b, k : k + 1] = value
        h_out[b] = h

    for_blocks(blocks, finish, unroll=1)


def run_force(entries, count, a, b, q, cot_x):
    blocks = cot_x.shape[0]
    smem = pl.BlockSpec(memory_space=pltpu.SMEM)
    vmem = pl.BlockSpec(memory_space=pltpu.VMEM)
    return pl.pallas_call(
        force_kernel,
        out_shape=(
            jax.ShapeDtypeStruct((blocks, 16, 128), F32),
            jax.ShapeDtypeStruct((blocks, 1, 128), F32),
        ),
        in_specs=[smem, smem] + [vmem] * 10,
        out_specs=(vmem, vmem),
        scratch_shapes=[
            pltpu.VMEM((3 * blocks, 48, 128), BF16),
            pltpu.VMEM((blocks + 1, 48, 128), BF16),
            pltpu.VMEM((3 * blocks, 2 * F_ROWS, 128), BF16),
            pltpu.VMEM((3 * blocks, 2 * C_ROWS, 128), BF16),
            pltpu.VMEM((blocks + 1, F_ROWS + C_ROWS, 128), F32),
            pltpu.VMEM((LONG // 2, 128, 256), F32),
            pltpu.VMEM((LONG, 256, 128), BF16),
            pltpu.VMEM((LONG, 256, 128), BF16),
        ],
        compiler_params=pltpu.CompilerParams(vmem_limit_bytes=58 << 20),
        name="force",
    )(entries, count, *a, *b, *q, cot_x)


def adjoint_kernel(
    entries, count, a_prev, a_own, a_next, h_prev, h_own, h_next, partial, occupied,
    gx_out, gm_out, sources, targets, channels, acc, distances, right,
):
    blocks = a_own.shape[0]
    for part, (a_ref, h_ref) in enumerate(((a_prev, h_prev), (a_own, h_own), (a_next, h_next))):

        def prepare(b, part=part, a_ref=a_ref, h_ref=h_ref):
            at = part * blocks + b
            a = a_ref[b]
            e = basis(a)
            sources[at] = source_features(e)
            channels[at] = stacked([h_ref[b] * e])
            if part == 1:
                targets[b] = target_features(target_basis(a))
                acc[b] = jnp.zeros((8, 128), F32)

        for_blocks(blocks, prepare)
    targets[blocks] = jnp.zeros((48, 128), BF16)
    acc[blocks] = jnp.zeros((8, 128), F32)

    def step(t):
        newest, oldest = group_at(entries, t, SHORT), group_at(entries, t - 2, SHORT)
        for k in range(0, SHORT, 2):
            for j in range(2):
                x, y = oldest[k + j]
                acc[x] = acc[x] + matrix_sum(channels[y], right[k + j])
            for j in range(2):
                c = distances[k // 2, :, 128 * j : 128 * j + 128]
                right[k + j] = split_rows(c * c)
            make_tiles(sources, targets, newest, k, distances)

    group_loop(count, SHORT, 3, step)

    def finish(b):
        a = a_own[b]
        s = acc[b]
        h = h_own[b]
        mass = a[5:6]
        grad_m = partial[b, 15:16] + KAPPA * jnp.sum(s * target_basis(a), axis=0, keepdims=True)
        gm_out[b] = grad_m * occupied[b]
        for k in range(3):
            pull = h * partial[b, 12 + k : 13 + k] + mass * (
                a[2 + k : 3 + k] * s[0:1] - s[2 + k : 3 + k]
            )
            gx_out[b, k : k + 1] = partial[b, 9 + k : 10 + k] - (6.0 * KAPPA) * pull

    for_blocks(blocks, finish, unroll=2)


def run_adjoint(entries, count, a, h, partial, occupied):
    blocks = partial.shape[0]
    smem = pl.BlockSpec(memory_space=pltpu.SMEM)
    vmem = pl.BlockSpec(memory_space=pltpu.VMEM)
    return pl.pallas_call(
        adjoint_kernel,
        out_shape=(
            jax.ShapeDtypeStruct((blocks, 3, 128), F32),
            jax.ShapeDtypeStruct((blocks, 1, 128), F32),
        ),
        in_specs=[smem, smem] + [vmem] * 8,
        out_specs=(vmem, vmem),
        scratch_shapes=[
            pltpu.VMEM((3 * blocks, 48, 128), BF16),
            pltpu.VMEM((blocks + 1, 48, 128), BF16),
            pltpu.VMEM((3 * blocks, 16, 128), BF16),
            pltpu.VMEM((blocks + 1, 8, 128), F32),
            pltpu.VMEM((SHORT // 2, 128, 256), F32),
            pltpu.VMEM((SHORT, 256, 128), BF16),
        ],
        compiler_params=pltpu.CompilerParams(vmem_limit_bytes=24 << 20),
        name="adjoint",
    )(entries, count, *a, *h, partial, occupied)


def shifted(value, by):
    devices = lax.axis_size("slab")
    pairs = [(i, i + by) for i in range(devices) if 0 <= i + by < devices]
    return lax.ppermute(value, "slab", pairs)


def around(value):
    return shifted(value, 1), value, shifted(value, -1)


def cube_root(mass):
    safe = jnp.where(mass > 0.0, mass, 1.0)
    root = jnp.exp(jnp.log(safe) * (1.0 / 3.0))
    root = root - (root * root * root - safe) / (3.0 * root * root)
    return jnp.where(mass > 0.0, root, 0.0)


def local(positions, velocity, masses, counts, pair_home, pair_far, pair_owner, cot_x, cot_v):
    occupied = (lax.broadcasted_iota(jnp.int32, masses.shape, 1) < counts[:, None]).astype(F32)
    mass = (masses * occupied)[:, None, :]
    norm = jnp.sum(positions * positions, axis=1, keepdims=True)
    one = jnp.ones_like(norm)
    a_own = jnp.concatenate(
        [one, norm, positions, mass, cube_root(mass), jnp.zeros_like(norm)], axis=1
    )
    g = DT * (cot_v + DT * cot_x)
    b_own = jnp.concatenate([velocity, g, jnp.zeros_like(g[:, :2])], axis=1)
    table = jnp.stack([pair_home, pair_far, pair_owner])
    p_table = shifted(table, 1)
    a = around(a_own)
    b = around(b_own)
    entries, count = make_list(
        pair_home, pair_far, pair_owner, p_table[0], p_table[1], p_table[2]
    )
    state = run_density(entries, count, *a)
    pq = state[:, :2]
    q = (shifted(pq, 1), state, shifted(pq, -1))
    partial, h = run_force(entries, count, a, b, q, cot_x)
    grad_x, grad_m = run_adjoint(entries, count, a, around(h), partial, occupied[:, None, :])
    return (partial[:, 0:3], partial[:, 3:6], grad_x, partial[:, 6:9], grad_m[:, 0])


def solution(mesh):
    block = P("slab", None, None)
    flat = P("slab")
    return jax.shard_map(
        local,
        mesh=mesh,
        in_specs=(block, block, P("slab", None), flat, flat, flat, flat, block, block),
        out_specs=(block, block, block, block, P("slab", None)),
        check_vma=False,
    )
```

```python
import functools

import jax
import jax.numpy as jnp
from jax import lax
from jax.experimental import pallas as pl
from jax.experimental.pallas import tpu as pltpu
from jax.sharding import PartitionSpec as P

DT = 0.1
GRAVITY = 1.0
KAPPA = 1.0 / 128.0
LEAD = 64
SHORT = 32
LONG = 32
F32 = jnp.float32
BF16 = jnp.bfloat16


def dot(a, b, ca=1, cb=0):
    return lax.dot_general(a, b, (((ca,), (cb,)), ((), ())), preferred_element_type=F32)


def rounded(value):
    return value.astype(BF16).astype(F32)


def halves(value):
    high = rounded(value)
    return high, value - high


def thirds(value):
    high = rounded(value)
    rest = value - high
    middle = rounded(rest)
    return high, middle, rest - middle


def source_features(e):
    h, m, l = thirds(e)
    return jnp.concatenate([h, h, m, h, l, m], axis=0).astype(BF16)


def target_features(r):
    h, m, l = thirds(r)
    return jnp.concatenate([h, m, h, l, h, m], axis=0).astype(BF16)


def row_index():
    return lax.broadcasted_iota(jnp.int32, (8, 128), 0)


def basis(a):
    return jnp.where(row_index() < 5, a, 0.0)


def target_basis(a):
    row = row_index()
    return jnp.where(
        row == 0, 1.0 - a[1:2], jnp.where(row == 1, -1.0, jnp.where(row < 5, 2.0 * a, 0.0))
    )


DEAD = 128 * 512 + 128


def tile_lists(home, far, owner):
    blocks, pairs = 128, home.shape[0]
    own = jnp.arange(blocks, dtype=jnp.int32)
    receiver = jnp.concatenate([own, home, far])
    key = jnp.concatenate(
        [own + blocks, far + blocks * (1 + owner), home + jnp.where(owner == 0, 1, 3) * blocks]
    )
    here = key < 3 * blocks
    order = jnp.arange(key.shape[0], dtype=jnp.int32)
    same = key[:, None] == key[None, :]
    less = key[None, :] < key[:, None]

    def count(mask):
        return jnp.sum(mask.astype(jnp.int32), axis=1)

    rank = count(same & (order[None, :] < order[:, None]))
    odd = (rank == 0) & (count(same) % 2 == 1)
    place = count(less) + rank + count(less & odd[None, :])
    size = jnp.sum((here & odd).astype(jnp.int32) + here.astype(jnp.int32))
    away = ~here
    size_away = jnp.sum((away & odd).astype(jnp.int32) + away.astype(jnp.int32))

    def placed(slots, start, value, default):
        slot = jnp.arange(slots, dtype=jnp.int32)
        hit = (place - start)[None, :] == slot[:, None]
        return default + jnp.sum(jnp.where(hit, (value - default)[None, :], 0), axis=1)

    capacity = blocks + 2 * pairs + 2 * blocks
    mine = placed(capacity, 0, jnp.where(here, receiver * 512 + key, DEAD), DEAD)
    away_slots = pairs + blocks
    theirs = jnp.stack(
        [
            placed(away_slots, size, receiver, 128),
            placed(away_slots, size, key - 3 * blocks, 128),
            jnp.broadcast_to(size_away, (away_slots,)),
        ]
    )
    return mine, size, theirs


def whole_list(mine, size, previous):
    codes = previous[0] * 512 + previous[1]
    tail = jnp.full((codes.shape[0] + 2 * LEAD,), DEAD, jnp.int32)
    entries = jnp.concatenate([tail[:LEAD], mine, tail])
    entries = lax.dynamic_update_slice(entries, codes, (LEAD + size,))
    return entries, jnp.broadcast_to(size + previous[2, 0], (8,))


def group_at(entries, t, size):
    twos = []
    for k in range(0, size, 2):
        first = entries[LEAD + t * size + k]
        second = entries[LEAD + t * size + k + 1]
        twos.append(
            (
                lax.shift_right_logical(first, 9),
                lax.shift_right_logical(second, 9),
                lax.bitwise_and(first, 511),
            )
        )
    return twos


def group_loop(count, size, stages, buffers, step):
    groups = lax.shift_right_logical(count[0] + (size - 1), size.bit_length() - 1)
    even, odd = buffers

    def body(half, carry):
        step(2 * half, even, odd)

        @pl.when(groups > 0)
        def _():
            step(2 * half + 1, odd, even)

        return carry

    lax.fori_loop(0, lax.shift_right_logical(groups + stages, 1), body, 0)


def make_tiles(sources, targets, two, distances, k):
    x0, x1, y = two
    right = jnp.concatenate([targets[x0], targets[x1]], axis=1)
    distances[k] = jnp.maximum(dot(sources[y], right, 0, 0), 0.0)


def add_both(acc, two, rows, total):
    acc[two[0], rows] = acc[two[0], rows] + total[:, :128]
    acc[two[1], rows] = acc[two[1], rows] + total[:, 128:]


def for_blocks(blocks, fn, unroll=4):
    def body(b, carry):
        fn(b)
        return carry

    lax.fori_loop(0, blocks, body, 0, unroll=unroll)


def density_kernel(
    entries, count, a_prev, a_own, a_next, out, rho_out, sources, targets, acc, *distances,
):
    blocks = a_own.shape[0]

    def prepare(b):
        for part, a_ref in enumerate((a_prev, a_own, a_next)):
            a = a_ref[b]
            sources[part * blocks + b] = source_features(basis(a) * a[6:7])
            if part == 1:
                targets[b] = target_features(target_basis(a))
                acc[b] = jnp.zeros((8, 128), F32)

    for_blocks(blocks, prepare, unroll=4)
    targets[blocks] = jnp.zeros((48, 128), BF16)
    acc[blocks] = jnp.zeros((8, 128), F32)

    def step(t, now, later):
        newer, older = group_at(entries, t, SHORT), group_at(entries, t - 1, SHORT)
        for k in range(SHORT // 2):
            c = now[k]
            mass_kernel = c * c * c
            total = jnp.sum(mass_kernel.reshape(16, 8, 256), axis=0)
            add_both(acc, older[k], slice(0, 8), total)
            make_tiles(sources, targets, newer[k], later, k)

    group_loop(count, SHORT, 2, distances, step)

    def finish(b):
        density = KAPPA * jnp.sum(acc[b], axis=0, keepdims=True)
        square = density * density + 0.25
        inverse = lax.rsqrt(square)
        inverse = inverse * (1.5 - 0.5 * square * inverse * inverse)
        bounded = square * inverse
        pressure = 0.5 * (bounded - inverse * inverse)
        out[b, 0:1] = pressure
        out[b, 1:2] = inverse
        rho_out[b] = density

    for_blocks(blocks, finish, unroll=8)


def run_density(entries, count, a_prev, a_own, a_next):
    blocks = a_own.shape[0]
    smem = pl.BlockSpec(memory_space=pltpu.SMEM)
    vmem = pl.BlockSpec(memory_space=pltpu.VMEM)
    return pl.pallas_call(
        density_kernel,
        out_shape=(
            jax.ShapeDtypeStruct((blocks, 2, 128), F32),
            jax.ShapeDtypeStruct((blocks, 1, 128), F32),
        ),
        in_specs=[smem, smem, vmem, vmem, vmem],
        out_specs=(vmem, vmem),
        scratch_shapes=[
            pltpu.VMEM((3 * blocks, 48, 128), BF16),
            pltpu.VMEM((blocks + 1, 48, 128), BF16),
            pltpu.VMEM((blocks + 1, 8, 128), F32),
        ]
        + [pltpu.VMEM((SHORT // 2, 128, 256), F32)] * 2,
        compiler_params=pltpu.CompilerParams(vmem_limit_bytes=58 << 20),
        name="density",
    )(entries, count, a_prev, a_own, a_next)


F_ROWS = 56
C_ROWS = 64


def stacked(groups):
    value = jnp.concatenate(groups, axis=0)
    high, low = halves(value)
    return jnp.concatenate([high, low], axis=0).astype(BF16)


def split_into(rights, distances, k, powers):
    for start in range(0, 128, 16):
        rows = slice(start, start + 16)
        c = distances[k, rows]
        for right, power in zip(rights, powers):
            value = c if power == 1 else c * c
            high = value.astype(BF16)
            right[k, rows] = high
            right[k, 128 + start : 144 + start] = (value - high.astype(F32)).astype(BF16)


def matrix_sum(channels, right):
    both = dot(jnp.concatenate([channels, channels], axis=1), right)
    rows = channels.shape[0] // 2
    return both[:rows] + both[rows:]


def pair_basis(a, p):
    row = row_index()
    e = basis(a)
    return jnp.where(row >= 5, p * pltpu.roll(e, 3, 0), jnp.where(row == 1, p, e))


def force_channels(a, b, p, q):
    row = row_index()
    x = [a[2 + k : 3 + k] for k in range(3)]
    mass, xg = a[5:6], a[7:8]
    first = jnp.where(row >= 4, (mass * q) * b, b)
    with_p = jnp.where(row < 3, p * b, jnp.where(row == 3, p * xg, 0.0))
    second = jnp.where(
        row == 0,
        mass,
        jnp.where(
            row < 4, mass * pltpu.roll(a, 7, 0), jnp.where(row < 7, pltpu.roll(b, 4, 0), xg)
        ),
    )
    second_p = p * second
    f = [first, a[1:2] * first] + [x[k] * first for k in range(3)]
    f += [mass * pair_basis(a, p), with_p]
    c = [second] + [x[k] * second for k in range(3)]
    c += [second_p] + [x[k] * second_p for k in range(3)]
    return stacked(f), stacked(c)


def force_kernel(
    entries, count, a_prev, a_own, a_next, b_prev, b_own, b_next, q_prev, q_own, q_next,
    rho, cot_x, x_out, v_out, gv_out, out, h_out, sources, targets, f_channels, c_channels, acc,
    *buffers,
):
    blocks = a_own.shape[0]
    row = row_index()
    parts = ((a_prev, b_prev, q_prev), (a_own, b_own, q_own), (a_next, b_next, q_next))

    def prepare(b):
        for part, (a_ref, b_ref, q_ref) in enumerate(parts):
            at = part * blocks + b
            a = a_ref[b]
            sources[at] = source_features(basis(a))
            f, c = force_channels(a, b_ref[b], q_ref[b, 0:1], q_ref[b, 1:2])
            f_channels[at] = f
            c_channels[at] = c
            if part == 1:
                targets[b] = target_features(target_basis(a))
                acc[b] = jnp.zeros((F_ROWS + C_ROWS, 128), F32)

    for_blocks(blocks, prepare, unroll=2)
    targets[blocks] = jnp.zeros((48, 128), BF16)
    acc[blocks] = jnp.zeros((F_ROWS + C_ROWS, 128), F32)

    def step(t, now, later):
        newest, oldest = group_at(entries, t, LONG), group_at(entries, t - 2, LONG)
        for k in range(LONG // 2):
            y = oldest[k][2]
            add_both(acc, oldest[k], slice(0, F_ROWS), matrix_sum(f_channels[y], now[1][k]))
            add_both(
                acc, oldest[k], slice(F_ROWS, F_ROWS + C_ROWS),
                matrix_sum(c_channels[y], now[2][k]),
            )
            split_into(later[1:], now[0], k, (2, 1))
            make_tiles(sources, targets, newest[k], later[0], k)

    group_loop(count, LONG, 3, (buffers[:3], buffers[3:]), step)

    def finish(b):
        a = a_own[b]
        bb = b_own[b]
        p, q = q_own[b, 0:1], q_own[b, 1:2]
        n = a[1:2]
        x = [a[2 + k : 3 + k] for k in range(3)]
        g = [bb[k : k + 1] for k in range(3)]
        v = [bb[5 + k : 6 + k] for k in range(3)]
        vg = bb[3:4]
        mass, xg = a[5:6], a[7:8]
        u = mass * q

        def group(k):
            return acc[b, 8 * k : 8 * k + 8]

        s_one, s_n = group(0), group(1)
        s_x = [group(2 + k) for k in range(3)]
        s_m, s_p = group(5), group(6)
        c_one, c_p = group(7), group(11)
        c_x = [group(8 + k) for k in range(3)]
        c_px = [group(12 + k) for k in range(3)]

        weighted = (
            (1.0 - n) * s_one - s_n + 2.0 * (x[0] * s_x[0] + x[1] * s_x[1] + x[2] * s_x[2])
        )
        w_g = [weighted[k : k + 1] for k in range(3)]
        w_u = weighted[4:5]
        energy = weighted[3:4] - (v[0] * w_g[0] + v[1] * w_g[1] + v[2] * w_g[2])
        m0, m1 = s_m[0:1], s_m[1:2]
        xm = [x[k] * m0 - s_m[2 + k : 3 + k] for k in range(3)]
        g0 = [s_one[k : k + 1] for k in range(3)]
        g1 = [s_p[k : k + 1] for k in range(3)]
        xg0 = s_x[0][0:1] + s_x[1][1:2] + s_x[2][2:3]
        xdg0 = x[0] * g0[0] + x[1] * g0[1] + x[2] * g0[2] - xg0
        xdg1 = x[0] * g1[0] + x[1] * g1[1] + x[2] * g1[2] - s_p[3:4]
        grad_m = KAPPA * (-6.0 * (p * xdg0 + xdg1) - 0.5 * q * energy)
        grad_q = (-0.5 * KAPPA) * mass * energy
        grad_p = (6.0 * KAPPA) * (g[0] * xm[0] + g[1] * xm[1] + g[2] * xm[2] - mass * xdg0)
        c_weight = 24.0 * jnp.where(
            row == 0,
            xg,
            jnp.where(
                row < 4,
                -pltpu.roll(bb, 1, 0),
                jnp.where(row < 7, -mass * pltpu.roll(a, 2, 0), mass),
            ),
        )
        f_weight = 3.0 * jnp.where(
            row < 3,
            u * pltpu.roll(bb, 3, 0),
            jnp.where(row == 3, -u, jnp.where(row == 4, -vg, pltpu.roll(bb, 5, 0))),
        )

        def through(c_sum, cp_sum, f_sum):
            return jnp.sum(
                c_weight * (p * c_sum + cp_sum) + f_weight * f_sum, axis=0, keepdims=True
            )

        through_one = through(c_one, c_p, s_one)
        at = pl.ds(b, 1)
        for k in range(3):
            accel = KAPPA * (
                6.0 * (p * xm[k] + x[k] * m1 - s_m[5 + k : 6 + k])
                + 0.5 * (weighted[5 + k : 6 + k] - v[k] * w_u)
            )
            if k == 2:
                accel = accel - GRAVITY
            new_v = v[k] + DT * accel
            v_out[k, at] = new_v
            x_out[k, at] = x[k] + DT * new_v
            gv_out[k, at] = g[k] * (1.0 / DT) - (0.5 * KAPPA) * (g[k] * w_u - u * w_g[k])
            direct = 6.0 * (g[k] * (p * m0 + m1) - mass * (p * g0[k] + g1[k]))
            out[b, k : k + 1] = cot_x[k, at] + KAPPA * (
                direct - x[k] * through_one + through(c_x[k], c_px[k], s_x[k])
            )
            out[b, 3 + k : 4 + k] = xm[k]
        out[b, 6:7] = grad_m
        h_out[b] = (rho[b] * q) * (
            0.5 * (1.0 + 2.0 * q * q * q) * grad_p - q * q * grad_q
        )

    for_blocks(blocks, finish, unroll=2)


def run_force(entries, count, a, b, q, rho, cot_x):
    blocks = rho.shape[0]
    smem = pl.BlockSpec(memory_space=pltpu.SMEM)
    vmem = pl.BlockSpec(memory_space=pltpu.VMEM)
    plane = jax.ShapeDtypeStruct((3, blocks, 128), F32)
    return pl.pallas_call(
        force_kernel,
        out_shape=(
            plane,
            plane,
            plane,
            jax.ShapeDtypeStruct((blocks, 8, 128), F32),
            jax.ShapeDtypeStruct((blocks, 1, 128), F32),
        ),
        in_specs=[smem, smem] + [vmem] * 11,
        out_specs=(vmem,) * 5,
        scratch_shapes=[
            pltpu.VMEM((3 * blocks, 48, 128), BF16),
            pltpu.VMEM((blocks + 1, 48, 128), BF16),
            pltpu.VMEM((3 * blocks, 2 * F_ROWS, 128), BF16),
            pltpu.VMEM((3 * blocks, 2 * C_ROWS, 128), BF16),
            pltpu.VMEM((blocks + 1, F_ROWS + C_ROWS, 128), F32),
        ]
        + [
            pltpu.VMEM((LONG // 2, 128, 256), F32),
            pltpu.VMEM((LONG // 2, 256, 256), BF16),
            pltpu.VMEM((LONG // 2, 256, 256), BF16),
        ]
        * 2,
        compiler_params=pltpu.CompilerParams(vmem_limit_bytes=58 << 20),
        name="force",
    )(entries, count, *a, *b, *q, rho, cot_x)


def adjoint_kernel(
    entries, count, a_prev, a_own, a_next, h_prev, h_own, h_next, partial, occupied,
    gx_out, gm_out, sources, targets, channels, acc, *buffers,
):
    blocks = a_own.shape[0]
    parts = ((a_prev, h_prev), (a_own, h_own), (a_next, h_next))

    def prepare(b):
        for part, (a_ref, h_ref) in enumerate(parts):
            at = part * blocks + b
            a = a_ref[b]
            e = basis(a)
            sources[at] = source_features(e)
            channels[at] = stacked([h_ref[b] * e])
            if part == 1:
                targets[b] = target_features(target_basis(a))
                acc[b] = jnp.zeros((8, 128), F32)

    for_blocks(blocks, prepare, unroll=4)
    targets[blocks] = jnp.zeros((48, 128), BF16)
    acc[blocks] = jnp.zeros((8, 128), F32)

    def step(t, now, later):
        newest, oldest = group_at(entries, t, SHORT), group_at(entries, t - 2, SHORT)
        for k in range(SHORT // 2):
            add_both(
                acc, oldest[k], slice(0, 8), matrix_sum(channels[oldest[k][2]], now[1][k])
            )
            split_into(later[1:], now[0], k, (2,))
            make_tiles(sources, targets, newest[k], later[0], k)

    group_loop(count, SHORT, 3, (buffers[:2], buffers[2:]), step)

    def finish(b):
        a = a_own[b]
        s = acc[b]
        h = h_own[b]
        mass = a[5:6]
        grad_m = partial[b, 6:7] + KAPPA * jnp.sum(s * target_basis(a), axis=0, keepdims=True)
        at = pl.ds(b, 1)
        gm_out[at] = grad_m * occupied[at]
        for k in range(3):
            pull = h * partial[b, 3 + k : 4 + k] + mass * (
                a[2 + k : 3 + k] * s[0:1] - s[2 + k : 3 + k]
            )
            gx_out[k, at] = partial[b, k : k + 1] - (6.0 * KAPPA) * pull

    for_blocks(blocks, finish, unroll=4)


def run_adjoint(entries, count, a, h, partial, occupied):
    blocks = partial.shape[0]
    smem = pl.BlockSpec(memory_space=pltpu.SMEM)
    vmem = pl.BlockSpec(memory_space=pltpu.VMEM)
    return pl.pallas_call(
        adjoint_kernel,
        out_shape=(
            jax.ShapeDtypeStruct((3, blocks, 128), F32),
            jax.ShapeDtypeStruct((blocks, 128), F32),
        ),
        in_specs=[smem, smem] + [vmem] * 8,
        out_specs=(vmem, vmem),
        scratch_shapes=[
            pltpu.VMEM((3 * blocks, 48, 128), BF16),
            pltpu.VMEM((blocks + 1, 48, 128), BF16),
            pltpu.VMEM((3 * blocks, 16, 128), BF16),
            pltpu.VMEM((blocks + 1, 8, 128), F32),
        ]
        + [
            pltpu.VMEM((SHORT // 2, 128, 256), F32),
            pltpu.VMEM((SHORT // 2, 256, 256), BF16),
        ]
        * 2,
        compiler_params=pltpu.CompilerParams(vmem_limit_bytes=58 << 20),
        name="adjoint",
    )(entries, count, *a, *h, partial, occupied)


def exchange_kernel(arrays, *refs):
    mine, previous, following = refs[:arrays], refs[arrays : 2 * arrays], refs[2 * arrays : 3 * arrays]
    send, receive = refs[3 * arrays :]
    devices = lax.axis_size("slab")
    me = lax.axis_index("slab")
    right, left = lax.rem(me + 1, devices), lax.rem(me + devices - 1, devices)
    mesh_id = pl.DeviceIdType.MESH
    barrier = pltpu.get_barrier_semaphore()
    for neighbour in (left, right):
        pl.semaphore_signal(barrier, inc=1, device_id=(neighbour,), device_id_type=mesh_id)
    pl.semaphore_wait(barrier, 2)
    copies = []
    for k in range(arrays):
        for way, (target, landing) in enumerate(((right, previous[k]), (left, following[k]))):
            copies.append(
                pltpu.make_async_remote_copy(
                    src_ref=mine[k],
                    dst_ref=landing,
                    send_sem=send.at[2 * k + way],
                    recv_sem=receive.at[2 * k + way],
                    device_id=(target,),
                    device_id_type=mesh_id,
                )
            )
            copies[-1].start()
    for copy in copies:
        copy.wait()


def exchange(identity, *values):
    count = len(values)
    anywhere = pl.BlockSpec(memory_space=pl.ANY)
    shapes = tuple(jax.ShapeDtypeStruct(v.shape, v.dtype) for v in values)
    got = pl.pallas_call(
        functools.partial(exchange_kernel, count),
        out_shape=shapes * 2,
        in_specs=[anywhere] * count,
        out_specs=(anywhere,) * (2 * count),
        scratch_shapes=[
            pltpu.SemaphoreType.DMA((2 * count,)),
            pltpu.SemaphoreType.DMA((2 * count,)),
        ],
        compiler_params=pltpu.CompilerParams(collective_id=identity, has_side_effects=True),
        name=f"exchange_{identity}",
    )(*values)
    return [(got[k], values[k], got[count + k]) for k in range(count)]


def cube_root(mass):
    safe = jnp.where(mass > 0.0, mass, 1.0)
    root = jnp.exp(jnp.log(safe) * (1.0 / 3.0))
    root = root - (root * root * root - safe) / (3.0 * root * root)
    return jnp.where(mass > 0.0, root, 0.0)


def local(positions, velocity, masses, counts, pair_home, pair_far, pair_owner, cot_x, cot_v):
    occupied = (lax.broadcasted_iota(jnp.int32, masses.shape, 1) < counts[:, None]).astype(F32)
    mass = (masses * occupied)[:, None, :]
    g = DT * (cot_v + DT * cot_x)

    def product(first, second):
        return jnp.sum(first * second, axis=1, keepdims=True)

    one = jnp.ones_like(mass)
    a_own = jnp.concatenate(
        [
            one, product(positions, positions), positions, mass, cube_root(mass),
            product(positions, g),
        ],
        axis=1,
    )
    b_own = jnp.concatenate([g, product(velocity, g), one, velocity], axis=1)
    mine, size, theirs = tile_lists(pair_home, pair_far, pair_owner)
    a, b, lists = exchange(0, a_own, b_own, theirs)
    entries, count = whole_list(mine, size, lists[0])
    pq, rho = run_density(entries, count, *a)
    (q,) = exchange(1, pq)
    planes = jnp.transpose(cot_x, (1, 0, 2))
    new_x, new_v, grad_v, partial, h = run_force(entries, count, a, b, q, rho, planes)
    (h_all,) = exchange(2, h)
    grad_x, grad_m = run_adjoint(entries, count, a, h_all, partial, occupied)

    def blocks_first(value):
        return jnp.transpose(value, (1, 0, 2))

    return (
        blocks_first(new_x), blocks_first(new_v), blocks_first(grad_x), blocks_first(grad_v),
        grad_m,
    )


def solution(mesh):
    block = P("slab", None, None)
    flat = P("slab")
    return jax.shard_map(
        local,
        mesh=mesh,
        in_specs=(block, block, P("slab", None), flat, flat, flat, flat, block, block),
        out_specs=(block, block, block, block, P("slab", None)),
        check_vma=False,
    )
```

```python
import functools

import jax
import jax.numpy as jnp
from jax import lax
from jax.experimental import pallas as pl
from jax.experimental.pallas import tpu as pltpu
from jax.sharding import PartitionSpec as P

DT = 0.1
GRAVITY = 1.0
KAPPA = 1.0 / 128.0
LEAD = 64
DENSE = 64
SHORT = 32
LONG = 32
F32 = jnp.float32
BF16 = jnp.bfloat16


def dot(a, b, ca=1, cb=0):
    return lax.dot_general(a, b, (((ca,), (cb,)), ((), ())), preferred_element_type=F32)


def rounded(value):
    return value.astype(BF16).astype(F32)


def halves(value):
    high = rounded(value)
    return high, value - high


def thirds(value):
    high = rounded(value)
    rest = value - high
    middle = rounded(rest)
    return high, middle, rest - middle


def source_features(e):
    h, m, l = thirds(e)
    return jnp.concatenate([h, h, m, h, l, m], axis=0).astype(BF16)


def target_features(r):
    h, m, l = thirds(r)
    return jnp.concatenate([h, m, h, l, h, m], axis=0).astype(BF16)


def row_index():
    return lax.broadcasted_iota(jnp.int32, (8, 128), 0)


def basis(a):
    return jnp.where(row_index() < 5, a, 0.0)


def target_basis(a):
    row = row_index()
    return jnp.where(
        row == 0, 1.0 - a[1:2], jnp.where(row == 1, -1.0, jnp.where(row < 5, 2.0 * a, 0.0))
    )


DEAD = 128 * 512 + 128


def tile_lists(home, far, owner):
    blocks, pairs = 128, home.shape[0]
    own = jnp.arange(blocks, dtype=jnp.int32)
    receiver = jnp.concatenate([own, home, far])
    key = jnp.concatenate(
        [own + blocks, far + blocks * (1 + owner), home + jnp.where(owner == 0, 1, 3) * blocks]
    )
    here = key < 3 * blocks
    order = jnp.arange(key.shape[0], dtype=jnp.int32)
    same = key[:, None] == key[None, :]
    less = key[None, :] < key[:, None]

    def count(mask):
        return jnp.sum(mask.astype(jnp.int32), axis=1)

    rank = count(same & (order[None, :] < order[:, None]))
    odd = (rank == 0) & (count(same) % 2 == 1)
    place = count(less) + rank + count(less & odd[None, :])
    size = jnp.sum((here & odd).astype(jnp.int32) + here.astype(jnp.int32))
    away = ~here
    size_away = jnp.sum((away & odd).astype(jnp.int32) + away.astype(jnp.int32))

    def placed(slots, start, value, default):
        slot = jnp.arange(slots, dtype=jnp.int32)
        hit = (place - start)[None, :] == slot[:, None]
        return default + jnp.sum(jnp.where(hit, (value - default)[None, :], 0), axis=1)

    capacity = blocks + 2 * pairs + 2 * blocks
    mine = placed(capacity, 0, jnp.where(here, receiver * 512 + key, DEAD), DEAD)
    away_slots = pairs + blocks
    theirs = jnp.stack(
        [
            placed(away_slots, size, receiver, 128),
            placed(away_slots, size, key - 3 * blocks, 128),
            jnp.broadcast_to(size_away, (away_slots,)),
        ]
    )
    return mine, size, theirs


def merge_lists(mine, sizes, previous, entries, count):
    size = sizes[0]
    theirs = previous[2, 0] * sizes[1]

    def chunks(length):
        return lax.shift_right_logical(length + 15, 4)

    for k in range(LEAD):
        entries[k] = DEAD

    def copy_mine(c, carry):
        for k in range(16):
            entries[LEAD + 16 * c + k] = mine[16 * c + k]
        return carry

    def copy_theirs(c, carry):
        for k in range(16):
            at = 16 * c + k
            entries[LEAD + size + at] = previous[0, at] * 512 + previous[1, at]
        return carry

    lax.fori_loop(0, chunks(size), copy_mine, 0)
    lax.fori_loop(0, chunks(theirs), copy_theirs, 0)
    for k in range(2 * LEAD):
        entries[LEAD + size + theirs + k] = DEAD
    count[0] = size + theirs


def group_at(entries, t, size):
    twos = []
    for k in range(0, size, 2):
        first = entries[LEAD + t * size + k]
        second = entries[LEAD + t * size + k + 1]
        twos.append(
            (
                lax.shift_right_logical(first, 9),
                lax.shift_right_logical(second, 9),
                lax.bitwise_and(first, 511),
            )
        )
    return twos


def group_loop(count, size, stages, buffers, step):
    groups = lax.shift_right_logical(count[0] + (size - 1), size.bit_length() - 1)
    even, odd = buffers

    def body(half, carry):
        step(2 * half, even, odd)

        @pl.when(2 * half + 1 < groups + (stages - 1))
        def _():
            step(2 * half + 1, odd, even)

        return carry

    lax.fori_loop(0, lax.shift_right_logical(groups + stages, 1), body, 0)


def make_tiles(sources, targets, two, distances, k):
    x0, x1, y = two
    right = jnp.concatenate([targets[x0], targets[x1]], axis=1)
    distances[k] = jnp.maximum(dot(sources[y], right, 0, 0), 0.0)


def add_both(acc, two, rows, total):
    acc[two[0], rows] = acc[two[0], rows] + total[:, :128]
    acc[two[1], rows] = acc[two[1], rows] + total[:, 128:]


def for_blocks(blocks, fn, unroll=4):
    def body(b, carry):
        fn(b)
        return carry

    lax.fori_loop(0, blocks, body, 0, unroll=unroll)


def density_kernel(
    mine, sizes, previous, a_prev, a_own, a_next, out, rho_out, entries, count,
    sources, targets, acc, *distances,
):
    blocks = a_own.shape[0]
    merge_lists(mine, sizes, previous, entries, count)

    def prepare(b):
        for part, a_ref in enumerate((a_prev, a_own, a_next)):
            a = a_ref[b]
            sources[part * blocks + b] = source_features(basis(a) * a[6:7])
            if part == 1:
                targets[b] = target_features(target_basis(a))
                acc[b] = jnp.zeros((8, 128), F32)

    for_blocks(blocks, prepare, unroll=4)
    targets[blocks] = jnp.zeros((48, 128), BF16)
    acc[blocks] = jnp.zeros((8, 128), F32)

    def step(t, now, later):
        newer, older = group_at(entries, t, DENSE), group_at(entries, t - 1, DENSE)
        for k in range(DENSE // 2):
            c = now[k]
            mass_kernel = c * c * c
            total = jnp.sum(mass_kernel.reshape(16, 8, 256), axis=0)
            add_both(acc, older[k], slice(0, 8), total)
            make_tiles(sources, targets, newer[k], later, k)

    group_loop(count, DENSE, 2, distances, step)

    def finish(b):
        density = KAPPA * jnp.sum(acc[b], axis=0, keepdims=True)
        square = density * density + 0.25
        inverse = lax.rsqrt(square)
        inverse = inverse * (1.5 - 0.5 * square * inverse * inverse)
        bounded = square * inverse
        pressure = 0.5 * (bounded - inverse * inverse)
        out[b, 0:1] = pressure
        out[b, 1:2] = inverse
        rho_out[b] = density

    for_blocks(blocks, finish, unroll=8)


def run_density(mine, sizes, previous, a_prev, a_own, a_next):
    blocks = a_own.shape[0]
    smem = pl.BlockSpec(memory_space=pltpu.SMEM)
    vmem = pl.BlockSpec(memory_space=pltpu.VMEM)
    return pl.pallas_call(
        density_kernel,
        out_shape=(
            jax.ShapeDtypeStruct((blocks, 2, 128), F32),
            jax.ShapeDtypeStruct((blocks, 1, 128), F32),
            jax.ShapeDtypeStruct((mine.shape[0] + previous.shape[1] + 3 * LEAD,), jnp.int32),
            jax.ShapeDtypeStruct((8,), jnp.int32),
        ),
        in_specs=[smem, smem, smem, vmem, vmem, vmem],
        out_specs=(vmem, vmem, smem, smem),
        scratch_shapes=[
            pltpu.VMEM((3 * blocks, 48, 128), BF16),
            pltpu.VMEM((blocks + 1, 48, 128), BF16),
            pltpu.VMEM((blocks + 1, 8, 128), F32),
        ]
        + [pltpu.VMEM((DENSE // 2, 128, 256), F32)] * 2,
        compiler_params=pltpu.CompilerParams(vmem_limit_bytes=58 << 20),
        name="density",
    )(mine, sizes, previous, a_prev, a_own, a_next)


F_ROWS = 56
C_ROWS = 64


def stacked(groups):
    value = jnp.concatenate(groups, axis=0)
    high, low = halves(value)
    return jnp.concatenate([high, low], axis=0).astype(BF16)


def split_into(rights, distances, k, powers):
    for start in range(0, 128, 16):
        rows = slice(start, start + 16)
        c = distances[k, rows]
        for right, power in zip(rights, powers):
            value = c if power == 1 else c * c
            high = value.astype(BF16)
            right[k, rows] = high
            right[k, 128 + start : 144 + start] = (value - high.astype(F32)).astype(BF16)


def matrix_sum(channels, right):
    both = dot(jnp.concatenate([channels, channels], axis=1), right)
    rows = channels.shape[0] // 2
    return both[:rows] + both[rows:]


def pair_basis(a, p):
    row = row_index()
    e = basis(a)
    return jnp.where(row >= 5, p * pltpu.roll(e, 3, 0), jnp.where(row == 1, p, e))


def force_channels(a, b, p, q):
    row = row_index()
    x = [a[2 + k : 3 + k] for k in range(3)]
    mass, xg = a[5:6], a[7:8]
    first = jnp.where(row >= 4, (mass * q) * b, b)
    with_p = jnp.where(row < 3, p * b, jnp.where(row == 3, p * xg, 0.0))
    second = jnp.where(
        row == 0,
        mass,
        jnp.where(
            row < 4, mass * pltpu.roll(a, 7, 0), jnp.where(row < 7, pltpu.roll(b, 4, 0), xg)
        ),
    )
    second_p = p * second
    f = [first, a[1:2] * first] + [x[k] * first for k in range(3)]
    f += [mass * pair_basis(a, p), with_p]
    c = [second] + [x[k] * second for k in range(3)]
    c += [second_p] + [x[k] * second_p for k in range(3)]
    return stacked(f), stacked(c)


def force_kernel(
    entries, count, a_prev, a_own, a_next, b_prev, b_own, b_next, q_prev, q_own, q_next,
    rho, cot_x, x_out, v_out, gv_out, out, h_out, sources, targets, f_channels, c_channels, acc,
    *buffers,
):
    blocks = a_own.shape[0]
    row = row_index()
    parts = ((a_prev, b_prev, q_prev), (a_own, b_own, q_own), (a_next, b_next, q_next))

    def prepare(b):
        for part, (a_ref, b_ref, q_ref) in enumerate(parts):
            at = part * blocks + b
            a = a_ref[b]
            sources[at] = source_features(basis(a))
            f, c = force_channels(a, b_ref[b], q_ref[b, 0:1], q_ref[b, 1:2])
            f_channels[at] = f
            c_channels[at] = c
            if part == 1:
                targets[b] = target_features(target_basis(a))
                acc[b] = jnp.zeros((F_ROWS + C_ROWS, 128), F32)

    for_blocks(blocks, prepare, unroll=2)
    targets[blocks] = jnp.zeros((48, 128), BF16)
    acc[blocks] = jnp.zeros((F_ROWS + C_ROWS, 128), F32)

    def step(t, now, later):
        newest, oldest = group_at(entries, t, LONG), group_at(entries, t - 2, LONG)
        for k in range(LONG // 2):
            y = oldest[k][2]
            add_both(acc, oldest[k], slice(0, F_ROWS), matrix_sum(f_channels[y], now[1][k]))
            add_both(
                acc, oldest[k], slice(F_ROWS, F_ROWS + C_ROWS),
                matrix_sum(c_channels[y], now[2][k]),
            )
            split_into(later[1:], now[0], k, (2, 1))
            make_tiles(sources, targets, newest[k], later[0], k)

    group_loop(count, LONG, 3, (buffers[:3], buffers[3:]), step)

    def finish(b):
        a = a_own[b]
        bb = b_own[b]
        p, q = q_own[b, 0:1], q_own[b, 1:2]
        n = a[1:2]
        x = [a[2 + k : 3 + k] for k in range(3)]
        g = [bb[k : k + 1] for k in range(3)]
        v = [bb[5 + k : 6 + k] for k in range(3)]
        vg = bb[3:4]
        mass, xg = a[5:6], a[7:8]
        u = mass * q

        def group(k):
            return acc[b, 8 * k : 8 * k + 8]

        s_one, s_n = group(0), group(1)
        s_x = [group(2 + k) for k in range(3)]
        s_m, s_p = group(5), group(6)
        c_one, c_p = group(7), group(11)
        c_x = [group(8 + k) for k in range(3)]
        c_px = [group(12 + k) for k in range(3)]

        weighted = (
            (1.0 - n) * s_one - s_n + 2.0 * (x[0] * s_x[0] + x[1] * s_x[1] + x[2] * s_x[2])
        )
        w_g = [weighted[k : k + 1] for k in range(3)]
        w_u = weighted[4:5]
        energy = weighted[3:4] - (v[0] * w_g[0] + v[1] * w_g[1] + v[2] * w_g[2])
        m0, m1 = s_m[0:1], s_m[1:2]
        xm = [x[k] * m0 - s_m[2 + k : 3 + k] for k in range(3)]
        g0 = [s_one[k : k + 1] for k in range(3)]
        g1 = [s_p[k : k + 1] for k in range(3)]
        xg0 = s_x[0][0:1] + s_x[1][1:2] + s_x[2][2:3]
        xdg0 = x[0] * g0[0] + x[1] * g0[1] + x[2] * g0[2] - xg0
        xdg1 = x[0] * g1[0] + x[1] * g1[1] + x[2] * g1[2] - s_p[3:4]
        grad_m = KAPPA * (-6.0 * (p * xdg0 + xdg1) - 0.5 * q * energy)
        grad_q = (-0.5 * KAPPA) * mass * energy
        grad_p = (6.0 * KAPPA) * (g[0] * xm[0] + g[1] * xm[1] + g[2] * xm[2] - mass * xdg0)
        c_weight = 24.0 * jnp.where(
            row == 0,
            xg,
            jnp.where(
                row < 4,
                -pltpu.roll(bb, 1, 0),
                jnp.where(row < 7, -mass * pltpu.roll(a, 2, 0), mass),
            ),
        )
        f_weight = 3.0 * jnp.where(
            row < 3,
            u * pltpu.roll(bb, 3, 0),
            jnp.where(row == 3, -u, jnp.where(row == 4, -vg, pltpu.roll(bb, 5, 0))),
        )

        def through(c_sum, cp_sum, f_sum):
            return jnp.sum(
                c_weight * (p * c_sum + cp_sum) + f_weight * f_sum, axis=0, keepdims=True
            )

        through_one = through(c_one, c_p, s_one)
        at = pl.ds(b, 1)
        for k in range(3):
            accel = KAPPA * (
                6.0 * (p * xm[k] + x[k] * m1 - s_m[5 + k : 6 + k])
                + 0.5 * (weighted[5 + k : 6 + k] - v[k] * w_u)
            )
            if k == 2:
                accel = accel - GRAVITY
            new_v = v[k] + DT * accel
            v_out[k, at] = new_v
            x_out[k, at] = x[k] + DT * new_v
            gv_out[k, at] = g[k] * (1.0 / DT) - (0.5 * KAPPA) * (g[k] * w_u - u * w_g[k])
            direct = 6.0 * (g[k] * (p * m0 + m1) - mass * (p * g0[k] + g1[k]))
            out[b, k : k + 1] = cot_x[k, at] + KAPPA * (
                direct - x[k] * through_one + through(c_x[k], c_px[k], s_x[k])
            )
            out[b, 3 + k : 4 + k] = xm[k]
        out[b, 6:7] = grad_m
        h_out[b] = (rho[b] * q) * (
            0.5 * (1.0 + 2.0 * q * q * q) * grad_p - q * q * grad_q
        )

    for_blocks(blocks, finish, unroll=2)


def run_force(entries, count, a, b, q, rho, cot_x):
    blocks = rho.shape[0]
    smem = pl.BlockSpec(memory_space=pltpu.SMEM)
    vmem = pl.BlockSpec(memory_space=pltpu.VMEM)
    plane = jax.ShapeDtypeStruct((3, blocks, 128), F32)
    return pl.pallas_call(
        force_kernel,
        out_shape=(
            plane,
            plane,
            plane,
            jax.ShapeDtypeStruct((blocks, 8, 128), F32),
            jax.ShapeDtypeStruct((blocks, 1, 128), F32),
        ),
        in_specs=[smem, smem] + [vmem] * 11,
        out_specs=(vmem,) * 5,
        scratch_shapes=[
            pltpu.VMEM((3 * blocks, 48, 128), BF16),
            pltpu.VMEM((blocks + 1, 48, 128), BF16),
            pltpu.VMEM((3 * blocks, 2 * F_ROWS, 128), BF16),
            pltpu.VMEM((3 * blocks, 2 * C_ROWS, 128), BF16),
            pltpu.VMEM((blocks + 1, F_ROWS + C_ROWS, 128), F32),
        ]
        + [
            pltpu.VMEM((LONG // 2, 128, 256), F32),
            pltpu.VMEM((LONG // 2, 256, 256), BF16),
            pltpu.VMEM((LONG // 2, 256, 256), BF16),
        ]
        * 2,
        compiler_params=pltpu.CompilerParams(vmem_limit_bytes=58 << 20),
        name="force",
    )(entries, count, *a, *b, *q, rho, cot_x)


def adjoint_kernel(
    entries, count, a_prev, a_own, a_next, h_prev, h_own, h_next, partial, occupied,
    gx_out, gm_out, sources, targets, channels, acc, *buffers,
):
    blocks = a_own.shape[0]
    parts = ((a_prev, h_prev), (a_own, h_own), (a_next, h_next))

    def prepare(b):
        for part, (a_ref, h_ref) in enumerate(parts):
            at = part * blocks + b
            a = a_ref[b]
            e = basis(a)
            sources[at] = source_features(e)
            channels[at] = stacked([h_ref[b] * e])
            if part == 1:
                targets[b] = target_features(target_basis(a))
                acc[b] = jnp.zeros((8, 128), F32)

    for_blocks(blocks, prepare, unroll=4)
    targets[blocks] = jnp.zeros((48, 128), BF16)
    acc[blocks] = jnp.zeros((8, 128), F32)

    def step(t, now, later):
        newest, oldest = group_at(entries, t, SHORT), group_at(entries, t - 2, SHORT)
        for k in range(SHORT // 2):
            add_both(
                acc, oldest[k], slice(0, 8), matrix_sum(channels[oldest[k][2]], now[1][k])
            )
            split_into(later[1:], now[0], k, (2,))
            make_tiles(sources, targets, newest[k], later[0], k)

    group_loop(count, SHORT, 3, (buffers[:2], buffers[2:]), step)

    def finish(b):
        a = a_own[b]
        s = acc[b]
        h = h_own[b]
        mass = a[5:6]
        grad_m = partial[b, 6:7] + KAPPA * jnp.sum(s * target_basis(a), axis=0, keepdims=True)
        at = pl.ds(b, 1)
        gm_out[at] = grad_m * occupied[at]
        for k in range(3):
            pull = h * partial[b, 3 + k : 4 + k] + mass * (
                a[2 + k : 3 + k] * s[0:1] - s[2 + k : 3 + k]
            )
            gx_out[k, at] = partial[b, k : k + 1] - (6.0 * KAPPA) * pull

    for_blocks(blocks, finish, unroll=4)


def run_adjoint(entries, count, a, h, partial, occupied):
    blocks = partial.shape[0]
    smem = pl.BlockSpec(memory_space=pltpu.SMEM)
    vmem = pl.BlockSpec(memory_space=pltpu.VMEM)
    return pl.pallas_call(
        adjoint_kernel,
        out_shape=(
            jax.ShapeDtypeStruct((3, blocks, 128), F32),
            jax.ShapeDtypeStruct((blocks, 128), F32),
        ),
        in_specs=[smem, smem] + [vmem] * 8,
        out_specs=(vmem, vmem),
        scratch_shapes=[
            pltpu.VMEM((3 * blocks, 48, 128), BF16),
            pltpu.VMEM((blocks + 1, 48, 128), BF16),
            pltpu.VMEM((3 * blocks, 16, 128), BF16),
            pltpu.VMEM((blocks + 1, 8, 128), F32),
        ]
        + [
            pltpu.VMEM((SHORT // 2, 128, 256), F32),
            pltpu.VMEM((SHORT // 2, 256, 256), BF16),
        ]
        * 2,
        compiler_params=pltpu.CompilerParams(vmem_limit_bytes=58 << 20),
        name="adjoint",
    )(entries, count, *a, *h, partial, occupied)


def exchange_kernel(arrays, *refs):
    mine, previous, following = refs[:arrays], refs[arrays : 2 * arrays], refs[2 * arrays : 3 * arrays]
    send, receive = refs[3 * arrays :]
    devices = lax.axis_size("slab")
    me = lax.axis_index("slab")
    mesh_id = pl.DeviceIdType.MESH
    barrier = pltpu.get_barrier_semaphore()
    has_left, has_right = me > 0, me < devices - 1
    left, right = lax.rem(me + devices - 1, devices), lax.rem(me + 1, devices)

    def copies(way):
        target, landing = ((right, previous), (left, following))[way]
        return [
            pltpu.make_async_remote_copy(
                src_ref=mine[k],
                dst_ref=landing[k],
                send_sem=send.at[2 * k + way],
                recv_sem=receive.at[2 * k + way],
                device_id=(target,),
                device_id_type=mesh_id,
            )
            for k in range(arrays)
        ]

    for there, neighbour in ((has_left, left), (has_right, right)):

        @pl.when(there)
        def _(neighbour=neighbour):
            pl.semaphore_signal(barrier, inc=1, device_id=(neighbour,), device_id_type=mesh_id)

    at_end = jnp.logical_or(me == 0, me == devices - 1)

    @pl.when(at_end)
    def _():
        pl.semaphore_wait(barrier, 1)

    @pl.when(jnp.logical_not(at_end))
    def _():
        pl.semaphore_wait(barrier, 2)

    for there, way in ((has_right, 0), (has_left, 1)):

        @pl.when(there)
        def _(way=way):
            for copy in copies(way):
                copy.start()

    for there, way in ((has_right, 0), (has_left, 1)):

        @pl.when(there)
        def _(way=way):
            for copy in copies(way):
                copy.wait_send()
            for copy in copies(1 - way):
                copy.wait_recv()


def exchange(identity, *values):
    count = len(values)
    anywhere = pl.BlockSpec(memory_space=pl.ANY)
    shapes = tuple(jax.ShapeDtypeStruct(v.shape, v.dtype) for v in values)
    got = pl.pallas_call(
        functools.partial(exchange_kernel, count),
        out_shape=shapes * 2,
        in_specs=[anywhere] * count,
        out_specs=(anywhere,) * (2 * count),
        scratch_shapes=[
            pltpu.SemaphoreType.DMA((2 * count,)),
            pltpu.SemaphoreType.DMA((2 * count,)),
        ],
        compiler_params=pltpu.CompilerParams(collective_id=identity, has_side_effects=True),
        name=f"exchange_{identity}",
    )(*values)
    return [(got[k], values[k], got[count + k]) for k in range(count)]


def cube_root(mass):
    safe = jnp.where(mass > 0.0, mass, 1.0)
    root = jnp.exp(jnp.log(safe) * (1.0 / 3.0))
    root = root - (root * root * root - safe) / (3.0 * root * root)
    return jnp.where(mass > 0.0, root, 0.0)


def local(positions, velocity, masses, counts, pair_home, pair_far, pair_owner, cot_x, cot_v):
    occupied = (lax.broadcasted_iota(jnp.int32, masses.shape, 1) < counts[:, None]).astype(F32)
    mass = (masses * occupied)[:, None, :]
    g = DT * (cot_v + DT * cot_x)

    def product(first, second):
        return jnp.sum(first * second, axis=1, keepdims=True)

    one = jnp.ones_like(mass)
    a_own = jnp.concatenate(
        [
            one, product(positions, positions), positions, mass, cube_root(mass),
            product(positions, g),
        ],
        axis=1,
    )
    b_own = jnp.concatenate([g, product(velocity, g), one, velocity], axis=1)
    mine, size, theirs = tile_lists(pair_home, pair_far, pair_owner)
    a, b, lists = exchange(0, a_own, b_own, theirs)
    has_previous = (lax.axis_index("slab") > 0).astype(jnp.int32)
    sizes = jnp.stack([size, has_previous])
    pq, rho, entries, count = run_density(mine, sizes, lists[0], *a)
    (q,) = exchange(1, pq)
    planes = jnp.transpose(cot_x, (1, 0, 2))
    new_x, new_v, grad_v, partial, h = run_force(entries, count, a, b, q, rho, planes)
    (h_all,) = exchange(2, h)
    grad_x, grad_m = run_adjoint(entries, count, a, h_all, partial, occupied)

    def blocks_first(value):
        return jnp.transpose(value, (1, 0, 2))

    return (
        blocks_first(new_x), blocks_first(new_v), blocks_first(grad_x), blocks_first(grad_v),
        grad_m,
    )


def solution(mesh):
    block = P("slab", None, None)
    flat = P("slab")
    return jax.shard_map(
        local,
        mesh=mesh,
        in_specs=(block, block, P("slab", None), flat, flat, flat, flat, block, block),
        out_specs=(block, block, block, block, P("slab", None)),
        check_vma=False,
    )
```

```python
import functools

import jax
import jax.numpy as jnp
from jax import lax
from jax.experimental import pallas as pl
from jax.experimental.pallas import tpu as pltpu
from jax.sharding import PartitionSpec as P

DT = 0.1
GRAVITY = 1.0
KAPPA = 1.0 / 128.0
LEAD = 128
DENSE = 64
SHORT = 64
LONG = 32
F32 = jnp.float32
BF16 = jnp.bfloat16


def dot(a, b, ca=1, cb=0):
    return lax.dot_general(a, b, (((ca,), (cb,)), ((), ())), preferred_element_type=F32)


def rounded(value):
    return value.astype(BF16).astype(F32)


def halves(value):
    high = rounded(value)
    return high, value - high


def thirds(value):
    high = rounded(value)
    rest = value - high
    middle = rounded(rest)
    return high, middle, rest - middle


def source_features(e):
    h, m, l = thirds(e)
    return jnp.concatenate([h, h, m, h, l, m], axis=0).astype(BF16)


def target_features(r):
    h, m, l = thirds(r)
    return jnp.concatenate([h, m, h, l, h, m], axis=0).astype(BF16)


def row_index():
    return lax.broadcasted_iota(jnp.int32, (8, 128), 0)


def rows_at(ref, b):
    return [ref[b, k : k + 1] for k in range(ref.shape[1])]


def rows_of(values):
    row = row_index()
    out = values[-1]
    for k in reversed(range(len(values) - 1)):
        out = jnp.where(row == k, values[k], out)
    return jnp.broadcast_to(out, (8, 128))


def inner(first, second):
    return first[0] * second[0] + first[1] * second[1] + first[2] * second[2]


def unpack(ref, b):
    rows = rows_at(ref, b)
    x, root = rows[:3], rows[3]
    return x, inner(x, x), root, root * root * root


def basis(x, norm):
    return rows_of([1.0, norm] + x + [0.0])


def target_basis(x, norm):
    return rows_of([1.0 - norm, -1.0] + [2.0 * value for value in x] + [0.0])


DEAD = 128 * 512 + 128


def tile_lists(home, far, owner):
    blocks, pairs = 128, home.shape[0]
    own = jnp.arange(blocks, dtype=jnp.int32)
    receiver = jnp.concatenate([own, home, far])
    key = jnp.concatenate(
        [own + blocks, far + blocks * (1 + owner), home + jnp.where(owner == 0, 1, 3) * blocks]
    )
    here = key < 3 * blocks
    order = jnp.arange(key.shape[0], dtype=jnp.int32)
    same = key[:, None] == key[None, :]
    less = key[None, :] < key[:, None]

    def count(mask):
        return jnp.sum(mask.astype(jnp.int32), axis=1)

    rank = count(same & (order[None, :] < order[:, None]))
    odd = (rank == 0) & (count(same) % 2 == 1)
    place = count(less) + rank + count(less & odd[None, :])
    size = jnp.sum((here & odd).astype(jnp.int32) + here.astype(jnp.int32))
    away = ~here
    size_away = jnp.sum((away & odd).astype(jnp.int32) + away.astype(jnp.int32))

    def placed(slots, start, value, default):
        slot = jnp.arange(slots, dtype=jnp.int32)
        hit = (place - start)[None, :] == slot[:, None]
        return default + jnp.sum(jnp.where(hit, (value - default)[None, :], 0), axis=1)

    capacity = blocks + 2 * pairs + 2 * blocks
    mine = placed(capacity, 0, jnp.where(here, receiver * 512 + key, DEAD), DEAD)
    away_slots = pairs + blocks
    theirs = jnp.stack(
        [
            placed(away_slots, size, receiver, 128),
            placed(away_slots, size, key - 3 * blocks, 128),
            jnp.broadcast_to(size_away, (away_slots,)),
        ]
    )
    return mine, size, theirs


def merge_lists(mine, sizes, previous, entries, count):
    size = sizes[0]
    theirs = previous[2, 0] * sizes[1]

    def chunks(length):
        return lax.shift_right_logical(length + 15, 4)

    for k in range(LEAD):
        entries[k] = DEAD

    def copy_mine(c, carry):
        for k in range(16):
            entries[LEAD + 16 * c + k] = mine[16 * c + k]
        return carry

    def copy_theirs(c, carry):
        for k in range(16):
            at = 16 * c + k
            entries[LEAD + size + at] = previous[0, at] * 512 + previous[1, at]
        return carry

    lax.fori_loop(0, chunks(size), copy_mine, 0)
    lax.fori_loop(0, chunks(theirs), copy_theirs, 0)
    for k in range(2 * LEAD):
        entries[LEAD + size + theirs + k] = DEAD
    count[0] = size + theirs


def group_at(entries, t, size):
    twos = []
    for k in range(0, size, 2):
        first = entries[LEAD + t * size + k]
        second = entries[LEAD + t * size + k + 1]
        twos.append(
            (
                lax.shift_right_logical(first, 9),
                lax.shift_right_logical(second, 9),
                lax.bitwise_and(first, 511),
            )
        )
    return twos


def group_loop(count, size, stages, buffers, step):
    groups = lax.shift_right_logical(count[0] + (size - 1), size.bit_length() - 1)
    even, odd = buffers

    def body(half, carry):
        step(2 * half, even, odd)

        @pl.when(2 * half + 1 < groups + (stages - 1))
        def _():
            step(2 * half + 1, odd, even)

        return carry

    lax.fori_loop(0, lax.shift_right_logical(groups + stages, 1), body, 0)


def make_tiles(sources, targets, two, distances, k):
    x0, x1, y = two
    right = jnp.concatenate([targets[x0], targets[x1]], axis=1)
    distances[k] = jnp.maximum(dot(sources[y], right, 0, 0), 0.0)


def add_both(acc, two, rows, total):
    acc[two[0], rows] = acc[two[0], rows] + total[:, :128]
    acc[two[1], rows] = acc[two[1], rows] + total[:, 128:]


def for_blocks(blocks, fn, unroll=4):
    def body(b, carry):
        fn(b)
        return carry

    lax.fori_loop(0, blocks, body, 0, unroll=unroll)


def density_kernel(
    mine, sizes, previous, a_prev, a_own, a_next, out, rho_out, entries, count,
    sources, targets, acc, *distances,
):
    blocks = a_own.shape[0]
    merge_lists(mine, sizes, previous, entries, count)

    def prepare(b):
        for part, a_ref in enumerate((a_prev, a_own, a_next)):
            x, norm, root, _ = unpack(a_ref, b)
            sources[part * blocks + b] = source_features(basis(x, norm) * root)
            if part == 1:
                targets[b] = target_features(target_basis(x, norm))
                acc[b] = jnp.zeros((8, 128), F32)

    for_blocks(blocks, prepare, unroll=4)
    targets[blocks] = jnp.zeros((48, 128), BF16)
    acc[blocks] = jnp.zeros((8, 128), F32)

    def step(t, now, later):
        newer, older = group_at(entries, t, DENSE), group_at(entries, t - 1, DENSE)
        for k in range(DENSE // 2):
            c = now[k]
            mass_kernel = c * c * c
            total = jnp.sum(mass_kernel.reshape(16, 8, 256), axis=0)
            add_both(acc, older[k], slice(0, 8), total)
            make_tiles(sources, targets, newer[k], later, k)

    group_loop(count, DENSE, 2, distances, step)

    def finish(b):
        density = KAPPA * jnp.sum(acc[b], axis=0, keepdims=True)
        square = density * density + 0.25
        inverse = lax.rsqrt(square)
        inverse = inverse * (1.5 - 0.5 * square * inverse * inverse)
        bounded = square * inverse
        pressure = 0.5 * (bounded - inverse * inverse)
        out[b, 0:1] = pressure
        out[b, 1:2] = inverse
        rho_out[b] = density

    for_blocks(blocks, finish, unroll=8)


def run_density(mine, sizes, previous, a_prev, a_own, a_next):
    blocks = a_own.shape[0]
    smem = pl.BlockSpec(memory_space=pltpu.SMEM)
    vmem = pl.BlockSpec(memory_space=pltpu.VMEM)
    return pl.pallas_call(
        density_kernel,
        out_shape=(
            jax.ShapeDtypeStruct((blocks, 2, 128), F32),
            jax.ShapeDtypeStruct((blocks, 1, 128), F32),
            jax.ShapeDtypeStruct((mine.shape[0] + previous.shape[1] + 3 * LEAD,), jnp.int32),
            jax.ShapeDtypeStruct((8,), jnp.int32),
        ),
        in_specs=[smem, smem, smem, vmem, vmem, vmem],
        out_specs=(vmem, vmem, smem, smem),
        scratch_shapes=[
            pltpu.VMEM((3 * blocks, 48, 128), BF16),
            pltpu.VMEM((blocks + 1, 48, 128), BF16),
            pltpu.VMEM((blocks + 1, 8, 128), F32),
        ]
        + [pltpu.VMEM((DENSE // 2, 128, 256), F32)] * 2,
        compiler_params=pltpu.CompilerParams(vmem_limit_bytes=58 << 20),
        name="density",
    )(mine, sizes, previous, a_prev, a_own, a_next)


F_ROWS = 56
C_ROWS = 64


def stacked(groups):
    value = jnp.concatenate(groups, axis=0)
    high, low = halves(value)
    return jnp.concatenate([high, low], axis=0).astype(BF16)


def split_into(rights, distances, k, powers):
    for start in range(0, 128, 16):
        rows = slice(start, start + 16)
        c = distances[k, rows]
        for right, power in zip(rights, powers):
            value = c if power == 1 else c * c
            high = value.astype(BF16)
            right[k, rows] = high
            right[k, 128 + start : 144 + start] = (value - high.astype(F32)).astype(BF16)


def matrix_sum(channels, right):
    both = dot(jnp.concatenate([channels, channels], axis=1), right)
    rows = channels.shape[0] // 2
    return both[:rows] + both[rows:]


def force_channels(x, norm, mass, v, g, p, q):
    u = mass * q
    xg = inner(x, g)
    px = [p * value for value in x]
    first = rows_of(g + [inner(v, g), u] + [u * value for value in v])
    with_p = rows_of([p * value for value in g] + [p * xg, 0.0])
    second = rows_of([mass] + [mass * value for value in x] + g + [xg])
    second_p = p * second
    f = [first, norm * first] + [value * first for value in x]
    f += [mass * rows_of([1.0, p] + x + px), with_p]
    c = [second] + [value * second for value in x]
    c += [second_p] + [value * second for value in px]
    return stacked(f), stacked(c)


def velocity_rows(b_ref, g_ref, b):
    rows, rest = rows_at(b_ref, b), rows_at(g_ref, b)
    return rows[:3], [rows[3]] + rest


def force_kernel(
    entries, count, a_prev, a_own, a_next, b_prev, b_own, b_next, g_prev, g_own, g_next,
    q_prev, q_own, q_next, rho, cot_x, x_out, v_out, gv_out, out, h_out, sources, targets, f_channels, c_channels, acc,
    *buffers,
):
    blocks = a_own.shape[0]
    parts = (
        (a_prev, b_prev, g_prev, q_prev),
        (a_own, b_own, g_own, q_own),
        (a_next, b_next, g_next, q_next),
    )

    def prepare(b):
        for part, (a_ref, b_ref, g_ref, q_ref) in enumerate(parts):
            at = part * blocks + b
            x, norm, _, mass = unpack(a_ref, b)
            v, g = velocity_rows(b_ref, g_ref, b)
            sources[at] = source_features(basis(x, norm))
            f, c = force_channels(x, norm, mass, v, g, q_ref[b, 0:1], q_ref[b, 1:2])
            f_channels[at] = f
            c_channels[at] = c
            if part == 1:
                targets[b] = target_features(target_basis(x, norm))
                acc[b] = jnp.zeros((F_ROWS + C_ROWS, 128), F32)

    for_blocks(blocks, prepare, unroll=2)
    targets[blocks] = jnp.zeros((48, 128), BF16)
    acc[blocks] = jnp.zeros((F_ROWS + C_ROWS, 128), F32)

    def step(t, now, later):
        newest, oldest = group_at(entries, t, LONG), group_at(entries, t - 2, LONG)
        for k in range(LONG // 2):
            y = oldest[k][2]
            add_both(acc, oldest[k], slice(0, F_ROWS), matrix_sum(f_channels[y], now[1][k]))
            add_both(
                acc, oldest[k], slice(F_ROWS, F_ROWS + C_ROWS),
                matrix_sum(c_channels[y], now[2][k]),
            )
            split_into(later[1:], now[0], k, (2, 1))
            make_tiles(sources, targets, newest[k], later[0], k)

    group_loop(count, LONG, 3, (buffers[:3], buffers[3:]), step)

    def finish(b):
        x, n, _, mass = unpack(a_own, b)
        v, g = velocity_rows(b_own, g_own, b)
        p, q = q_own[b, 0:1], q_own[b, 1:2]
        vg, xg = inner(v, g), inner(x, g)
        u = mass * q

        def group(k):
            return acc[b, 8 * k : 8 * k + 8]

        s_one, s_n = group(0), group(1)
        s_x = [group(2 + k) for k in range(3)]
        s_m, s_p = group(5), group(6)
        c_one, c_p = group(7), group(11)
        c_x = [group(8 + k) for k in range(3)]
        c_px = [group(12 + k) for k in range(3)]

        weighted = (
            (1.0 - n) * s_one - s_n + 2.0 * (x[0] * s_x[0] + x[1] * s_x[1] + x[2] * s_x[2])
        )
        w_g = [weighted[k : k + 1] for k in range(3)]
        w_u = weighted[4:5]
        energy = weighted[3:4] - (v[0] * w_g[0] + v[1] * w_g[1] + v[2] * w_g[2])
        m0, m1 = s_m[0:1], s_m[1:2]
        xm = [x[k] * m0 - s_m[2 + k : 3 + k] for k in range(3)]
        g0 = [s_one[k : k + 1] for k in range(3)]
        g1 = [s_p[k : k + 1] for k in range(3)]
        xg0 = s_x[0][0:1] + s_x[1][1:2] + s_x[2][2:3]
        xdg0 = x[0] * g0[0] + x[1] * g0[1] + x[2] * g0[2] - xg0
        xdg1 = x[0] * g1[0] + x[1] * g1[1] + x[2] * g1[2] - s_p[3:4]
        grad_m = KAPPA * (-6.0 * (p * xdg0 + xdg1) - 0.5 * q * energy)
        grad_q = (-0.5 * KAPPA) * mass * energy
        grad_p = (6.0 * KAPPA) * (g[0] * xm[0] + g[1] * xm[1] + g[2] * xm[2] - mass * xdg0)
        mass24 = 24.0 * mass
        c_weight = rows_of(
            [24.0 * xg] + [-24.0 * value for value in g] + [-mass24 * value for value in x]
            + [mass24]
        )
        u3 = 3.0 * u
        f_weight = rows_of(
            [u3 * value for value in v] + [-u3, -3.0 * vg] + [3.0 * value for value in g]
        )

        def through(c_sum, cp_sum, f_sum):
            return jnp.sum(
                c_weight * (p * c_sum + cp_sum) + f_weight * f_sum, axis=0, keepdims=True
            )

        through_one = through(c_one, c_p, s_one)
        at = pl.ds(b, 1)
        for k in range(3):
            accel = KAPPA * (
                6.0 * (p * xm[k] + x[k] * m1 - s_m[5 + k : 6 + k])
                + 0.5 * (weighted[5 + k : 6 + k] - v[k] * w_u)
            )
            if k == 2:
                accel = accel - GRAVITY
            new_v = v[k] + DT * accel
            v_out[k, at] = new_v
            x_out[k, at] = x[k] + DT * new_v
            gv_out[k, at] = g[k] * (1.0 / DT) - (0.5 * KAPPA) * (g[k] * w_u - u * w_g[k])
            direct = 6.0 * (g[k] * (p * m0 + m1) - mass * (p * g0[k] + g1[k]))
            out[b, k : k + 1] = cot_x[k, at] + KAPPA * (
                direct - x[k] * through_one + through(c_x[k], c_px[k], s_x[k])
            )
            out[b, 3 + k : 4 + k] = xm[k]
        out[b, 6:7] = grad_m
        h_out[b] = (rho[b] * q) * (
            0.5 * (1.0 + 2.0 * q * q * q) * grad_p - q * q * grad_q
        )

    for_blocks(blocks, finish, unroll=2)


def run_force(entries, count, a, b, g, q, rho, cot_x):
    blocks = rho.shape[0]
    smem = pl.BlockSpec(memory_space=pltpu.SMEM)
    vmem = pl.BlockSpec(memory_space=pltpu.VMEM)
    plane = jax.ShapeDtypeStruct((3, blocks, 128), F32)
    return pl.pallas_call(
        force_kernel,
        out_shape=(
            plane,
            plane,
            plane,
            jax.ShapeDtypeStruct((blocks, 8, 128), F32),
            jax.ShapeDtypeStruct((blocks, 1, 128), F32),
        ),
        in_specs=[smem, smem] + [vmem] * 14,
        out_specs=(vmem,) * 5,
        scratch_shapes=[
            pltpu.VMEM((3 * blocks, 48, 128), BF16),
            pltpu.VMEM((blocks + 1, 48, 128), BF16),
            pltpu.VMEM((3 * blocks, 2 * F_ROWS, 128), BF16),
            pltpu.VMEM((3 * blocks, 2 * C_ROWS, 128), BF16),
            pltpu.VMEM((blocks + 1, F_ROWS + C_ROWS, 128), F32),
        ]
        + [
            pltpu.VMEM((LONG // 2, 128, 256), F32),
            pltpu.VMEM((LONG // 2, 256, 256), BF16),
            pltpu.VMEM((LONG // 2, 256, 256), BF16),
        ]
        * 2,
        compiler_params=pltpu.CompilerParams(vmem_limit_bytes=58 << 20),
        name="force",
    )(entries, count, *a, *b, *g, *q, rho, cot_x)


def adjoint_kernel(
    entries, count, a_prev, a_own, a_next, h_prev, h_own, h_next, partial, occupied,
    gx_out, gm_out, sources, targets, channels, acc, *buffers,
):
    blocks = a_own.shape[0]
    parts = ((a_prev, h_prev), (a_own, h_own), (a_next, h_next))

    def prepare(b):
        for part, (a_ref, h_ref) in enumerate(parts):
            at = part * blocks + b
            x, norm, _, _ = unpack(a_ref, b)
            e = basis(x, norm)
            sources[at] = source_features(e)
            channels[at] = stacked([h_ref[b] * e])
            if part == 1:
                targets[b] = target_features(target_basis(x, norm))
                acc[b] = jnp.zeros((8, 128), F32)

    for_blocks(blocks, prepare, unroll=4)
    targets[blocks] = jnp.zeros((48, 128), BF16)
    acc[blocks] = jnp.zeros((8, 128), F32)

    def step(t, now, later):
        newest, oldest = group_at(entries, t, SHORT), group_at(entries, t - 2, SHORT)
        for k in range(SHORT // 2):
            add_both(
                acc, oldest[k], slice(0, 8), matrix_sum(channels[oldest[k][2]], now[1][k])
            )
            split_into(later[1:], now[0], k, (2,))
            make_tiles(sources, targets, newest[k], later[0], k)

    group_loop(count, SHORT, 3, (buffers[:2], buffers[2:]), step)

    def finish(b):
        x, norm, _, mass = unpack(a_own, b)
        s = acc[b]
        h = h_own[b]
        grad_m = partial[b, 6:7] + KAPPA * jnp.sum(
            s * target_basis(x, norm), axis=0, keepdims=True
        )
        at = pl.ds(b, 1)
        gm_out[at] = grad_m * occupied[at]
        for k in range(3):
            pull = h * partial[b, 3 + k : 4 + k] + mass * (
                x[k] * s[0:1] - s[2 + k : 3 + k]
            )
            gx_out[k, at] = partial[b, k : k + 1] - (6.0 * KAPPA) * pull

    for_blocks(blocks, finish, unroll=4)


def run_adjoint(entries, count, a, h, partial, occupied):
    blocks = partial.shape[0]
    smem = pl.BlockSpec(memory_space=pltpu.SMEM)
    vmem = pl.BlockSpec(memory_space=pltpu.VMEM)
    return pl.pallas_call(
        adjoint_kernel,
        out_shape=(
            jax.ShapeDtypeStruct((3, blocks, 128), F32),
            jax.ShapeDtypeStruct((blocks, 128), F32),
        ),
        in_specs=[smem, smem] + [vmem] * 8,
        out_specs=(vmem, vmem),
        scratch_shapes=[
            pltpu.VMEM((3 * blocks, 48, 128), BF16),
            pltpu.VMEM((blocks + 1, 48, 128), BF16),
            pltpu.VMEM((3 * blocks, 16, 128), BF16),
            pltpu.VMEM((blocks + 1, 8, 128), F32),
        ]
        + [
            pltpu.VMEM((SHORT // 2, 128, 256), F32),
            pltpu.VMEM((SHORT // 2, 256, 256), BF16),
        ]
        * 2,
        compiler_params=pltpu.CompilerParams(vmem_limit_bytes=58 << 20),
        name="adjoint",
    )(entries, count, *a, *h, partial, occupied)


def exchange_kernel(arrays, *refs):
    mine, previous, following = refs[:arrays], refs[arrays : 2 * arrays], refs[2 * arrays : 3 * arrays]
    send, receive = refs[3 * arrays :]
    devices = lax.axis_size("slab")
    me = lax.axis_index("slab")
    mesh_id = pl.DeviceIdType.MESH
    barrier = pltpu.get_barrier_semaphore()
    has_left, has_right = me > 0, me < devices - 1
    left, right = lax.rem(me + devices - 1, devices), lax.rem(me + 1, devices)

    def copies(way):
        target, landing = ((right, previous), (left, following))[way]
        return [
            pltpu.make_async_remote_copy(
                src_ref=mine[k],
                dst_ref=landing[k],
                send_sem=send.at[2 * k + way],
                recv_sem=receive.at[2 * k + way],
                device_id=(target,),
                device_id_type=mesh_id,
            )
            for k in range(arrays)
        ]

    for there, neighbour in ((has_left, left), (has_right, right)):

        @pl.when(there)
        def _(neighbour=neighbour):
            pl.semaphore_signal(barrier, inc=1, device_id=(neighbour,), device_id_type=mesh_id)

    at_end = jnp.logical_or(me == 0, me == devices - 1)

    @pl.when(at_end)
    def _():
        pl.semaphore_wait(barrier, 1)

    @pl.when(jnp.logical_not(at_end))
    def _():
        pl.semaphore_wait(barrier, 2)

    for there, way in ((has_right, 0), (has_left, 1)):

        @pl.when(there)
        def _(way=way):
            for copy in copies(way):
                copy.start()

    for there, way in ((has_right, 0), (has_left, 1)):

        @pl.when(there)
        def _(way=way):
            for copy in copies(way):
                copy.wait_send()
            for copy in copies(1 - way):
                copy.wait_recv()


def exchange(identity, *values):
    count = len(values)
    anywhere = pl.BlockSpec(memory_space=pl.ANY)
    shapes = tuple(jax.ShapeDtypeStruct(v.shape, v.dtype) for v in values)
    got = pl.pallas_call(
        functools.partial(exchange_kernel, count),
        out_shape=shapes * 2,
        in_specs=[anywhere] * count,
        out_specs=(anywhere,) * (2 * count),
        scratch_shapes=[
            pltpu.SemaphoreType.DMA((2 * count,)),
            pltpu.SemaphoreType.DMA((2 * count,)),
        ],
        compiler_params=pltpu.CompilerParams(collective_id=identity, has_side_effects=True),
        name=f"exchange_{identity}",
    )(*values)
    return [(got[k], values[k], got[count + k]) for k in range(count)]


def cube_root(mass):
    safe = jnp.where(mass > 0.0, mass, 1.0)
    root = jnp.exp(jnp.log(safe) * (1.0 / 3.0))
    root = root - (root * root * root - safe) / (3.0 * root * root)
    return jnp.where(mass > 0.0, root, 0.0)


def local(positions, velocity, masses, counts, pair_home, pair_far, pair_owner, cot_x, cot_v):
    occupied = (lax.broadcasted_iota(jnp.int32, masses.shape, 1) < counts[:, None]).astype(F32)
    mass = (masses * occupied)[:, None, :]
    g = DT * (cot_v + DT * cot_x)

    a_own = jnp.concatenate([positions, cube_root(mass)], axis=1)
    b_own = jnp.concatenate([velocity, g[:, 0:1]], axis=1)
    mine, size, theirs = tile_lists(pair_home, pair_far, pair_owner)
    a, b, rest, lists = exchange(0, a_own, b_own, g[:, 1:3], theirs)
    has_previous = (lax.axis_index("slab") > 0).astype(jnp.int32)
    sizes = jnp.stack([size, has_previous])
    pq, rho, entries, count = run_density(mine, sizes, lists[0], *a)
    (q,) = exchange(1, pq)
    planes = jnp.transpose(cot_x, (1, 0, 2))
    new_x, new_v, grad_v, partial, h = run_force(entries, count, a, b, rest, q, rho, planes)
    (h_all,) = exchange(2, h)
    grad_x, grad_m = run_adjoint(entries, count, a, h_all, partial, occupied)

    def blocks_first(value):
        return jnp.transpose(value, (1, 0, 2))

    return (
        blocks_first(new_x), blocks_first(new_v), blocks_first(grad_x), blocks_first(grad_v),
        grad_m,
    )


def solution(mesh):
    block = P("slab", None, None)
    flat = P("slab")
    return jax.shard_map(
        local,
        mesh=mesh,
        in_specs=(block, block, P("slab", None), flat, flat, flat, flat, block, block),
        out_specs=(block, block, block, block, P("slab", None)),
        check_vma=False,
    )
```

```python
import functools

import jax
import jax.numpy as jnp
from jax import lax
from jax.experimental import pallas as pl
from jax.experimental.pallas import tpu as pltpu
from jax.sharding import PartitionSpec as P

DT = 0.1
GRAVITY = 1.0
KAPPA = 1.0 / 128.0
LEAD = 128
DENSE = 128
SHORT = 64
LONG = 32
F32 = jnp.float32
BF16 = jnp.bfloat16


def dot(a, b, ca=1, cb=0):
    return lax.dot_general(a, b, (((ca,), (cb,)), ((), ())), preferred_element_type=F32)


def rounded(value):
    return value.astype(BF16).astype(F32)


def halves(value):
    high = rounded(value)
    return high, value - high


def thirds(value):
    high = rounded(value)
    rest = value - high
    middle = rounded(rest)
    return high, middle, rest - middle


def source_features(e):
    h, m, l = thirds(e)
    return jnp.concatenate([h, h, m, h, l, m], axis=0).astype(BF16)


def target_features(r):
    h, m, l = thirds(r)
    return jnp.concatenate([h, m, h, l, h, m], axis=0).astype(BF16)


def row_index():
    return lax.broadcasted_iota(jnp.int32, (8, 128), 0)


def rows_at(ref, b):
    return [ref[b, k : k + 1] for k in range(ref.shape[1])]


def rows_of(values):
    row = row_index()
    out = values[-1]
    for k in reversed(range(len(values) - 1)):
        out = jnp.where(row == k, values[k], out)
    return jnp.broadcast_to(out, (8, 128))


def inner(first, second):
    return first[0] * second[0] + first[1] * second[1] + first[2] * second[2]


def unpack(ref, b):
    rows = rows_at(ref, b)
    x, root = rows[:3], rows[3]
    return x, inner(x, x), root, root * root * root


def basis(x, norm):
    return rows_of([1.0, norm] + x + [0.0])


def target_basis(x, norm):
    return rows_of([1.0 - norm, -1.0] + [2.0 * value for value in x] + [0.0])


DEAD = 128 * 512 + 128


def tile_lists(home, far, owner):
    blocks, pairs = 128, home.shape[0]
    own = jnp.arange(blocks, dtype=jnp.int32)
    receiver = jnp.concatenate([own, home, far])
    key = jnp.concatenate(
        [own + blocks, far + blocks * (1 + owner), home + jnp.where(owner == 0, 1, 3) * blocks]
    )
    here = key < 3 * blocks
    order = jnp.arange(key.shape[0], dtype=jnp.int32)
    same = key[:, None] == key[None, :]
    less = key[None, :] < key[:, None]

    def count(mask):
        return jnp.sum(mask.astype(jnp.int32), axis=1)

    rank = count(same & (order[None, :] < order[:, None]))
    odd = (rank == 0) & (count(same) % 2 == 1)
    place = count(less) + rank + count(less & odd[None, :])
    size = jnp.sum((here & odd).astype(jnp.int32) + here.astype(jnp.int32))
    away = ~here
    size_away = jnp.sum((away & odd).astype(jnp.int32) + away.astype(jnp.int32))

    def placed(slots, start, value, default):
        slot = jnp.arange(slots, dtype=jnp.int32)
        hit = (place - start)[None, :] == slot[:, None]
        return default + jnp.sum(jnp.where(hit, (value - default)[None, :], 0), axis=1)

    capacity = blocks + 2 * pairs + 2 * blocks
    mine = placed(capacity, 0, jnp.where(here, receiver * 512 + key, DEAD), DEAD)
    away_slots = pairs + blocks
    theirs = jnp.stack(
        [
            placed(away_slots, size, receiver, 128),
            placed(away_slots, size, key - 3 * blocks, 128),
            jnp.broadcast_to(size_away, (away_slots,)),
        ]
    )
    return mine, size, theirs


def merge_lists(mine, sizes, previous, entries, count):
    size = sizes[0]
    theirs = previous[2, 0] * sizes[1]

    def chunks(length):
        return lax.shift_right_logical(length + 15, 4)

    for k in range(LEAD):
        entries[k] = DEAD

    def copy_mine(c, carry):
        for k in range(16):
            entries[LEAD + 16 * c + k] = mine[16 * c + k]
        return carry

    def copy_theirs(c, carry):
        for k in range(16):
            at = 16 * c + k
            entries[LEAD + size + at] = previous[0, at] * 512 + previous[1, at]
        return carry

    lax.fori_loop(0, chunks(size), copy_mine, 0)
    lax.fori_loop(0, chunks(theirs), copy_theirs, 0)
    for k in range(2 * LEAD):
        entries[LEAD + size + theirs + k] = DEAD
    count[0] = size + theirs


def group_at(entries, t, size):
    twos = []
    for k in range(0, size, 2):
        first = entries[LEAD + t * size + k]
        second = entries[LEAD + t * size + k + 1]
        twos.append(
            (
                lax.shift_right_logical(first, 9),
                lax.shift_right_logical(second, 9),
                lax.bitwise_and(first, 511),
            )
        )
    return twos


def group_loop(count, size, stages, buffers, step):
    groups = lax.shift_right_logical(count[0] + (size - 1), size.bit_length() - 1)
    even, odd = buffers

    def body(half, carry):
        step(2 * half, even, odd)

        @pl.when(2 * half + 1 < groups + (stages - 1))
        def _():
            step(2 * half + 1, odd, even)

        return carry

    lax.fori_loop(0, lax.shift_right_logical(groups + stages, 1), body, 0)


def make_tiles(sources, targets, two, distances, k):
    x0, x1, y = two
    right = jnp.concatenate([targets[x0], targets[x1]], axis=1)
    distances[k] = jnp.maximum(dot(sources[y], right, 0, 0), 0.0)


def add_both(acc, two, rows, total):
    acc[two[0], rows] = acc[two[0], rows] + total[:, :128]
    acc[two[1], rows] = acc[two[1], rows] + total[:, 128:]


def for_blocks(blocks, fn, unroll=4):
    def body(b, carry):
        fn(b)
        return carry

    lax.fori_loop(0, blocks, body, 0, unroll=unroll)


def density_kernel(
    mine, sizes, previous, a_prev, a_own, a_next, out, rho_out, entries, count,
    sources, targets, acc, *distances,
):
    blocks = a_own.shape[0]
    merge_lists(mine, sizes, previous, entries, count)

    def prepare(b):
        for part, a_ref in enumerate((a_prev, a_own, a_next)):
            x, norm, root, _ = unpack(a_ref, b)
            sources[part * blocks + b] = source_features(basis(x, norm) * root)
            if part == 1:
                targets[b] = target_features(target_basis(x, norm))
                acc[b] = jnp.zeros((8, 128), F32)

    for_blocks(blocks, prepare, unroll=4)
    targets[blocks] = jnp.zeros((48, 128), BF16)
    acc[blocks] = jnp.zeros((8, 128), F32)

    def step(t, now, later):
        newer, older = group_at(entries, t, DENSE), group_at(entries, t - 1, DENSE)
        for k in range(DENSE // 2):
            c = now[k]
            mass_kernel = c * c * c
            total = jnp.sum(mass_kernel.reshape(16, 8, 256), axis=0)
            add_both(acc, older[k], slice(0, 8), total)
            make_tiles(sources, targets, newer[k], later, k)

    group_loop(count, DENSE, 2, distances, step)

    def finish(b):
        density = KAPPA * jnp.sum(acc[b], axis=0, keepdims=True)
        square = density * density + 0.25
        inverse = lax.rsqrt(square)
        inverse = inverse * (1.5 - 0.5 * square * inverse * inverse)
        bounded = square * inverse
        pressure = 0.5 * (bounded - inverse * inverse)
        out[b, 0:1] = pressure
        out[b, 1:2] = inverse
        rho_out[b] = density

    for_blocks(blocks, finish, unroll=8)


def run_density(mine, sizes, previous, a_prev, a_own, a_next):
    blocks = a_own.shape[0]
    smem = pl.BlockSpec(memory_space=pltpu.SMEM)
    vmem = pl.BlockSpec(memory_space=pltpu.VMEM)
    return pl.pallas_call(
        density_kernel,
        out_shape=(
            jax.ShapeDtypeStruct((blocks, 2, 128), F32),
            jax.ShapeDtypeStruct((blocks, 1, 128), F32),
            jax.ShapeDtypeStruct((mine.shape[0] + previous.shape[1] + 3 * LEAD,), jnp.int32),
            jax.ShapeDtypeStruct((8,), jnp.int32),
        ),
        in_specs=[smem, smem, smem, vmem, vmem, vmem],
        out_specs=(vmem, vmem, smem, smem),
        scratch_shapes=[
            pltpu.VMEM((3 * blocks, 48, 128), BF16),
            pltpu.VMEM((blocks + 1, 48, 128), BF16),
            pltpu.VMEM((blocks + 1, 8, 128), F32),
        ]
        + [pltpu.VMEM((DENSE // 2, 128, 256), F32)] * 2,
        compiler_params=pltpu.CompilerParams(vmem_limit_bytes=58 << 20),
        name="density",
    )(mine, sizes, previous, a_prev, a_own, a_next)


F_ROWS = 56
C_ROWS = 64


def stacked(groups):
    value = jnp.concatenate(groups, axis=0)
    high, low = halves(value)
    return jnp.concatenate([high, low], axis=0).astype(BF16)


def split_into(rights, distances, k, powers):
    for start in range(0, 128, 16):
        rows = slice(start, start + 16)
        c = distances[k, rows]
        for right, power in zip(rights, powers):
            value = c if power == 1 else c * c
            high = value.astype(BF16)
            right[k, rows] = high
            right[k, 128 + start : 144 + start] = (value - high.astype(F32)).astype(BF16)


def matrix_sum(channels, right):
    both = dot(jnp.concatenate([channels, channels], axis=1), right)
    rows = channels.shape[0] // 2
    return both[:rows] + both[rows:]


def force_channels(x, norm, mass, v, g, p, q):
    u = mass * q
    xg = inner(x, g)
    px = [p * value for value in x]
    first = rows_of(g + [inner(v, g), u] + [u * value for value in v])
    with_p = rows_of([p * value for value in g] + [p * xg, 0.0])
    second = rows_of([mass] + [mass * value for value in x] + g + [xg])
    second_p = p * second
    f = [first, norm * first] + [value * first for value in x]
    f += [mass * rows_of([1.0, p] + x + px), with_p]
    c = [second] + [value * second for value in x]
    c += [second_p] + [value * second for value in px]
    return stacked(f), stacked(c)


def velocity_rows(b_ref, g_ref, b):
    rows, rest = rows_at(b_ref, b), rows_at(g_ref, b)
    return rows[:3], [rows[3]] + rest


def force_kernel(
    entries, count, a_prev, a_own, a_next, b_prev, b_own, b_next, g_prev, g_own, g_next,
    q_prev, q_own, q_next, rho, cot_x, x_out, v_out, gv_out, out, h_out, sources, targets, f_channels, c_channels, acc,
    *buffers,
):
    blocks = a_own.shape[0]
    parts = (
        (a_prev, b_prev, g_prev, q_prev),
        (a_own, b_own, g_own, q_own),
        (a_next, b_next, g_next, q_next),
    )

    def prepare(b):
        for part, (a_ref, b_ref, g_ref, q_ref) in enumerate(parts):
            at = part * blocks + b
            x, norm, _, mass = unpack(a_ref, b)
            v, g = velocity_rows(b_ref, g_ref, b)
            sources[at] = source_features(basis(x, norm))
            f, c = force_channels(x, norm, mass, v, g, q_ref[b, 0:1], q_ref[b, 1:2])
            f_channels[at] = f
            c_channels[at] = c
            if part == 1:
                targets[b] = target_features(target_basis(x, norm))
                acc[b] = jnp.zeros((F_ROWS + C_ROWS, 128), F32)

    for_blocks(blocks, prepare, unroll=2)
    targets[blocks] = jnp.zeros((48, 128), BF16)
    acc[blocks] = jnp.zeros((F_ROWS + C_ROWS, 128), F32)

    def step(t, now, later):
        newest, oldest = group_at(entries, t, LONG), group_at(entries, t - 2, LONG)
        for k in range(LONG // 2):
            y = oldest[k][2]
            add_both(acc, oldest[k], slice(0, F_ROWS), matrix_sum(f_channels[y], now[1][k]))
            add_both(
                acc, oldest[k], slice(F_ROWS, F_ROWS + C_ROWS),
                matrix_sum(c_channels[y], now[2][k]),
            )
            split_into(later[1:], now[0], k, (2, 1))
            make_tiles(sources, targets, newest[k], later[0], k)

    group_loop(count, LONG, 3, (buffers[:3], buffers[3:]), step)

    def finish(b):
        x, n, _, mass = unpack(a_own, b)
        v, g = velocity_rows(b_own, g_own, b)
        p, q = q_own[b, 0:1], q_own[b, 1:2]
        vg, xg = inner(v, g), inner(x, g)
        u = mass * q

        def group(k):
            return acc[b, 8 * k : 8 * k + 8]

        s_one, s_n = group(0), group(1)
        s_x = [group(2 + k) for k in range(3)]
        s_m, s_p = group(5), group(6)
        c_one, c_p = group(7), group(11)
        c_x = [group(8 + k) for k in range(3)]
        c_px = [group(12 + k) for k in range(3)]

        weighted = (
            (1.0 - n) * s_one - s_n + 2.0 * (x[0] * s_x[0] + x[1] * s_x[1] + x[2] * s_x[2])
        )
        w_g = [weighted[k : k + 1] for k in range(3)]
        w_u = weighted[4:5]
        energy = weighted[3:4] - (v[0] * w_g[0] + v[1] * w_g[1] + v[2] * w_g[2])
        m0, m1 = s_m[0:1], s_m[1:2]
        xm = [x[k] * m0 - s_m[2 + k : 3 + k] for k in range(3)]
        g0 = [s_one[k : k + 1] for k in range(3)]
        g1 = [s_p[k : k + 1] for k in range(3)]
        xg0 = s_x[0][0:1] + s_x[1][1:2] + s_x[2][2:3]
        xdg0 = x[0] * g0[0] + x[1] * g0[1] + x[2] * g0[2] - xg0
        xdg1 = x[0] * g1[0] + x[1] * g1[1] + x[2] * g1[2] - s_p[3:4]
        grad_m = KAPPA * (-6.0 * (p * xdg0 + xdg1) - 0.5 * q * energy)
        grad_q = (-0.5 * KAPPA) * mass * energy
        grad_p = (6.0 * KAPPA) * (g[0] * xm[0] + g[1] * xm[1] + g[2] * xm[2] - mass * xdg0)
        mass24 = 24.0 * mass
        c_weight = rows_of(
            [24.0 * xg] + [-24.0 * value for value in g] + [-mass24 * value for value in x]
            + [mass24]
        )
        u3 = 3.0 * u
        f_weight = rows_of(
            [u3 * value for value in v] + [-u3, -3.0 * vg] + [3.0 * value for value in g]
        )

        def through(c_sum, cp_sum, f_sum):
            return jnp.sum(
                c_weight * (p * c_sum + cp_sum) + f_weight * f_sum, axis=0, keepdims=True
            )

        through_one = through(c_one, c_p, s_one)
        at = pl.ds(b, 1)
        for k in range(3):
            accel = KAPPA * (
                6.0 * (p * xm[k] + x[k] * m1 - s_m[5 + k : 6 + k])
                + 0.5 * (weighted[5 + k : 6 + k] - v[k] * w_u)
            )
            if k == 2:
                accel = accel - GRAVITY
            new_v = v[k] + DT * accel
            v_out[k, at] = new_v
            x_out[k, at] = x[k] + DT * new_v
            gv_out[k, at] = g[k] * (1.0 / DT) - (0.5 * KAPPA) * (g[k] * w_u - u * w_g[k])
            direct = 6.0 * (g[k] * (p * m0 + m1) - mass * (p * g0[k] + g1[k]))
            out[b, k : k + 1] = cot_x[k, at] + KAPPA * (
                direct - x[k] * through_one + through(c_x[k], c_px[k], s_x[k])
            )
            out[b, 3 + k : 4 + k] = xm[k]
        out[b, 6:7] = grad_m
        h_out[b] = (rho[b] * q) * (
            0.5 * (1.0 + 2.0 * q * q * q) * grad_p - q * q * grad_q
        )

    for_blocks(blocks, finish, unroll=2)


def run_force(entries, count, a, b, g, q, rho, cot_x):
    blocks = rho.shape[0]
    smem = pl.BlockSpec(memory_space=pltpu.SMEM)
    vmem = pl.BlockSpec(memory_space=pltpu.VMEM)
    plane = jax.ShapeDtypeStruct((3, blocks, 128), F32)
    return pl.pallas_call(
        force_kernel,
        out_shape=(
            plane,
            plane,
            plane,
            jax.ShapeDtypeStruct((blocks, 8, 128), F32),
            jax.ShapeDtypeStruct((blocks, 1, 128), F32),
        ),
        in_specs=[smem, smem] + [vmem] * 14,
        out_specs=(vmem,) * 5,
        scratch_shapes=[
            pltpu.VMEM((3 * blocks, 48, 128), BF16),
            pltpu.VMEM((blocks + 1, 48, 128), BF16),
            pltpu.VMEM((3 * blocks, 2 * F_ROWS, 128), BF16),
            pltpu.VMEM((3 * blocks, 2 * C_ROWS, 128), BF16),
            pltpu.VMEM((blocks + 1, F_ROWS + C_ROWS, 128), F32),
        ]
        + [
            pltpu.VMEM((LONG // 2, 128, 256), F32),
            pltpu.VMEM((LONG // 2, 256, 256), BF16),
            pltpu.VMEM((LONG // 2, 256, 256), BF16),
        ]
        * 2,
        compiler_params=pltpu.CompilerParams(vmem_limit_bytes=58 << 20),
        name="force",
    )(entries, count, *a, *b, *g, *q, rho, cot_x)


def adjoint_kernel(
    entries, count, a_prev, a_own, a_next, h_prev, h_own, h_next, partial, occupied,
    gx_out, gm_out, sources, targets, channels, acc, *buffers,
):
    blocks = a_own.shape[0]
    parts = ((a_prev, h_prev), (a_own, h_own), (a_next, h_next))

    def prepare(b):
        for part, (a_ref, h_ref) in enumerate(parts):
            at = part * blocks + b
            x, norm, _, _ = unpack(a_ref, b)
            e = basis(x, norm)
            sources[at] = source_features(e)
            channels[at] = stacked([h_ref[b] * e])
            if part == 1:
                targets[b] = target_features(target_basis(x, norm))
                acc[b] = jnp.zeros((8, 128), F32)

    for_blocks(blocks, prepare, unroll=4)
    targets[blocks] = jnp.zeros((48, 128), BF16)
    acc[blocks] = jnp.zeros((8, 128), F32)

    def step(t, now, later):
        newest, oldest = group_at(entries, t, SHORT), group_at(entries, t - 2, SHORT)
        for k in range(SHORT // 2):
            add_both(
                acc, oldest[k], slice(0, 8), matrix_sum(channels[oldest[k][2]], now[1][k])
            )
            split_into(later[1:], now[0], k, (2,))
            make_tiles(sources, targets, newest[k], later[0], k)

    group_loop(count, SHORT, 3, (buffers[:2], buffers[2:]), step)

    def finish(b):
        x, norm, _, mass = unpack(a_own, b)
        s = acc[b]
        h = h_own[b]
        grad_m = partial[b, 6:7] + KAPPA * jnp.sum(
            s * target_basis(x, norm), axis=0, keepdims=True
        )
        at = pl.ds(b, 1)
        gm_out[at] = grad_m * occupied[at]
        for k in range(3):
            pull = h * partial[b, 3 + k : 4 + k] + mass * (
                x[k] * s[0:1] - s[2 + k : 3 + k]
            )
            gx_out[k, at] = partial[b, k : k + 1] - (6.0 * KAPPA) * pull

    for_blocks(blocks, finish, unroll=4)


def run_adjoint(entries, count, a, h, partial, occupied):
    blocks = partial.shape[0]
    smem = pl.BlockSpec(memory_space=pltpu.SMEM)
    vmem = pl.BlockSpec(memory_space=pltpu.VMEM)
    return pl.pallas_call(
        adjoint_kernel,
        out_shape=(
            jax.ShapeDtypeStruct((3, blocks, 128), F32),
            jax.ShapeDtypeStruct((blocks, 128), F32),
        ),
        in_specs=[smem, smem] + [vmem] * 8,
        out_specs=(vmem, vmem),
        scratch_shapes=[
            pltpu.VMEM((3 * blocks, 48, 128), BF16),
            pltpu.VMEM((blocks + 1, 48, 128), BF16),
            pltpu.VMEM((3 * blocks, 16, 128), BF16),
            pltpu.VMEM((blocks + 1, 8, 128), F32),
        ]
        + [
            pltpu.VMEM((SHORT // 2, 128, 256), F32),
            pltpu.VMEM((SHORT // 2, 256, 256), BF16),
        ]
        * 2,
        compiler_params=pltpu.CompilerParams(vmem_limit_bytes=58 << 20),
        name="adjoint",
    )(entries, count, *a, *h, partial, occupied)


def exchange_kernel(arrays, *refs):
    mine, previous, following = refs[:arrays], refs[arrays : 2 * arrays], refs[2 * arrays : 3 * arrays]
    send, receive = refs[3 * arrays :]
    devices = lax.axis_size("slab")
    me = lax.axis_index("slab")
    mesh_id = pl.DeviceIdType.MESH
    barrier = pltpu.get_barrier_semaphore()
    has_left, has_right = me > 0, me < devices - 1
    left, right = lax.rem(me + devices - 1, devices), lax.rem(me + 1, devices)

    def copies(way):
        target, landing = ((right, previous), (left, following))[way]
        return [
            pltpu.make_async_remote_copy(
                src_ref=mine[k],
                dst_ref=landing[k],
                send_sem=send.at[2 * k + way],
                recv_sem=receive.at[2 * k + way],
                device_id=(target,),
                device_id_type=mesh_id,
            )
            for k in range(arrays)
        ]

    for there, neighbour in ((has_left, left), (has_right, right)):

        @pl.when(there)
        def _(neighbour=neighbour):
            pl.semaphore_signal(barrier, inc=1, device_id=(neighbour,), device_id_type=mesh_id)

    at_end = jnp.logical_or(me == 0, me == devices - 1)

    @pl.when(at_end)
    def _():
        pl.semaphore_wait(barrier, 1)

    @pl.when(jnp.logical_not(at_end))
    def _():
        pl.semaphore_wait(barrier, 2)

    for there, way in ((has_right, 0), (has_left, 1)):

        @pl.when(there)
        def _(way=way):
            for copy in copies(way):
                copy.start()

    for there, way in ((has_right, 0), (has_left, 1)):

        @pl.when(there)
        def _(way=way):
            for copy in copies(way):
                copy.wait_send()
            for copy in copies(1 - way):
                copy.wait_recv()


def exchange(identity, *values):
    count = len(values)
    anywhere = pl.BlockSpec(memory_space=pl.ANY)
    shapes = tuple(jax.ShapeDtypeStruct(v.shape, v.dtype) for v in values)
    got = pl.pallas_call(
        functools.partial(exchange_kernel, count),
        out_shape=shapes * 2,
        in_specs=[anywhere] * count,
        out_specs=(anywhere,) * (2 * count),
        scratch_shapes=[
            pltpu.SemaphoreType.DMA((2 * count,)),
            pltpu.SemaphoreType.DMA((2 * count,)),
        ],
        compiler_params=pltpu.CompilerParams(collective_id=identity, has_side_effects=True),
        name=f"exchange_{identity}",
    )(*values)
    return [(got[k], values[k], got[count + k]) for k in range(count)]


def cube_root(mass):
    safe = jnp.where(mass > 0.0, mass, 1.0)
    root = jnp.exp(jnp.log(safe) * (1.0 / 3.0))
    root = root - (root * root * root - safe) / (3.0 * root * root)
    return jnp.where(mass > 0.0, root, 0.0)


def local(positions, velocity, masses, counts, pair_home, pair_far, pair_owner, cot_x, cot_v):
    occupied = (lax.broadcasted_iota(jnp.int32, masses.shape, 1) < counts[:, None]).astype(F32)
    mass = (masses * occupied)[:, None, :]
    g = DT * (cot_v + DT * cot_x)

    a_own = jnp.concatenate([positions, cube_root(mass)], axis=1)
    b_own = jnp.concatenate([velocity, g[:, 0:1]], axis=1)
    mine, size, theirs = tile_lists(pair_home, pair_far, pair_owner)
    a, b, rest, lists = exchange(0, a_own, b_own, g[:, 1:3], theirs)
    has_previous = (lax.axis_index("slab") > 0).astype(jnp.int32)
    sizes = jnp.stack([size, has_previous])
    pq, rho, entries, count = run_density(mine, sizes, lists[0], *a)
    (q,) = exchange(1, pq)
    planes = jnp.transpose(cot_x, (1, 0, 2))
    new_x, new_v, grad_v, partial, h = run_force(entries, count, a, b, rest, q, rho, planes)
    (h_all,) = exchange(2, h)
    grad_x, grad_m = run_adjoint(entries, count, a, h_all, partial, occupied)

    def blocks_first(value):
        return jnp.transpose(value, (1, 0, 2))

    return (
        blocks_first(new_x), blocks_first(new_v), blocks_first(grad_x), blocks_first(grad_v),
        grad_m,
    )


def solution(mesh):
    block = P("slab", None, None)
    flat = P("slab")
    return jax.shard_map(
        local,
        mesh=mesh,
        in_specs=(block, block, P("slab", None), flat, flat, flat, flat, block, block),
        out_specs=(block, block, block, block, P("slab", None)),
        check_vma=False,
    )
```
